512 devices in a mesh: dp: 4 (over y), ctx: 64 (over x, z), mp: 2 (over core).
Axes of the slice: x: 4, y: 4, z: 16, core: 2. Of those that a mesh axis runs over, the one named last changes fastest.
Arguments:
- features: bfloat16 [4, 8192, 3, 4096], P('dp', 'ctx', None, 'mp'), may hold values from -6 to 6
- conv_weight: float32 [7, 3, 4096], P(None, None, 'mp'), may hold values from -2 to 2
- log_rate: float32 [8, 32], P(None, 'mp'), as said below
- residues: float32 [8, 4096], P(None, 'mp'), may hold values from -4 to 4
- skip_weight: float32 [4096], P('mp'), may hold values from 0.5 to 1.5
- norm_gain: float32 [4096], P('mp'), may hold values from 0.5 to 1.5
- cotangent: bfloat16 [4, 8192, 4096], P('dp', 'ctx', 'mp'), may hold values from -6 to 6
Outputs:
- block_out: bfloat16 [4, 8192, 4096], P('dp', 'ctx', 'mp')
- feature_grad: bfloat16 [4, 8192, 3, 4096], P('dp', 'ctx', None, 'mp')
- conv_grad: float32 [7, 3, 4096], P(None, None, 'mp')
- rate_grad: float32 [8, 32], P(None, 'mp')
- residue_grad: float32 [8, 4096], P(None, 'mp')
- skip_grad: float32 [4096], P('mp')
- gain_grad: float32 [4096], P('mp')
The draws below stay inside these ranges and needn't reach their ends.
Inputs may be any that keep to these rules, and one draw needn't show every extreme that they name: log_rate lies between ln(1 / 1048576) and ln(1 / 16).
All inputs are finite; a program needn't handle non-finite values.
Results may differ from the reference program's by a relative error of at most 0.0011.
Values may be sent and summed in bfloat16 or wider, within the bound.
No kernel may reach another device: no remote copies, remote signals or barrier semaphores. Data moves between devices by JAX's collectives and lax.ppermute only.
A program may use at most 128 MiB of HBM per device.

```python
import math
import jax
import jax.numpy as jnp
from jax import lax

D = 4096
GROUPS = 32
POLES = 8
WIDTH = 7
TOK_DEV = 128
SEQS = 4
LENGTH = 8192
GSIZE = 128
N_CTX = 64


def rate_table(key):
    stream = jax.random.fold_in(key, 11)
    key_slow = jax.random.fold_in(stream, 0)
    lowest = -math.log(128.0 * LENGTH)
    highest = -math.log(16.0)
    return jax.random.uniform(key_slow, (POLES, GROUPS), jnp.float32, lowest, highest)


def draw_log_rate(key, part):
    return rate_table(key)


def draw_residues(key, part):
    rate_values = jnp.exp(rate_table(key))
    floor_rate = jnp.maximum(rate_values, 1.0 / LENGTH)
    spread = jnp.repeat(jnp.sqrt(2.0 * floor_rate / POLES), D // GROUPS, axis=1)
    channel = jnp.power(10.0, jnp.arange(D, dtype=jnp.float32) / D)
    noise_key = jax.random.fold_in(key, 23)
    noise_draw = jax.random.truncated_normal(noise_key, -4.0, 4.0, (POLES, D), jnp.float32)
    return noise_draw * spread * channel


def shard_levels(own_key, shape, shards, smallest, high):
    def one(axis_at, shards_of):
        heights = jax.random.uniform(jax.random.fold_in(jax.random.fold_in(own_key, 6), axis_at), (shards_of,), jnp.float32, smallest / len(shards), high / len(shards))
        return jnp.repeat(jnp.exp(heights), shape[axis_at] // shards_of).reshape((-1,) + (1,) * (len(shape) - axis_at - 1))

    level = one(*shards[0])
    for cut in shards[1:]:
        level = level * one(*cut)
    return level


def normal_values(key, extent, width, reach, cuts=(), kind=jnp.bfloat16):
    loudness = shard_levels(key, extent, cuts, -0.22, 0.18) if cuts else 1.0
    drawn = jax.random.normal(key, extent, jnp.float32) * width * loudness
    return jnp.minimum(jnp.maximum(drawn, -reach), reach).astype(kind)


def setup_inputs(seed: int = 0) -> dict:
    arg_keys = jax.random.split(jax.random.key(seed), 8)
    features = normal_values(arg_keys[0], (SEQS, LENGTH, 3, D), 1.0, 6.0, ((0, 4), (1, 64), (3, 2)))
    conv_weight = normal_values(arg_keys[1], (WIDTH, 3, D), WIDTH ** -0.5, 2.0, ((2, 2),), jnp.float32)
    log_rate = draw_log_rate(jax.random.fold_in(arg_keys[7], 71), 0)
    residues = draw_residues(jax.random.fold_in(arg_keys[7], 71), 0)
    skip_weight = jnp.clip(0.5 + 1.0 * jax.random.uniform(arg_keys[4], (D,), jnp.float32) ** shard_levels(arg_keys[4], (D,), ((0, 2),), -0.2, 0.2), 0.5, 1.5)
    norm_gain = jnp.clip(1.0 + 0.1 * jax.random.normal(arg_keys[5], (D,), jnp.float32), 0.5, 1.5)
    cotangent = normal_values(arg_keys[6], (SEQS, LENGTH, D), 1.0, 6.0, ((0, 4), (1, 64), (2, 2)))
    return {"features": features, "conv_weight": conv_weight, "log_rate": log_rate, "residues": residues, "skip_weight": skip_weight, "norm_gain": norm_gain, "cotangent": cotangent}


EPSILON = 1e-06
HIGHEST = lax.Precision.HIGHEST

def short_filter(seq_feats, conv_weight):
    halo_rows = WIDTH - 1
    padded = jnp.concatenate([jnp.zeros((halo_rows, 3, D), jnp.float32), seq_feats], axis=0)
    running = jnp.zeros((LENGTH, 3, D), jnp.float32)
    for offset in range(WIDTH):
        running = running + conv_weight[offset] * padded[halo_rows - offset:halo_rows - offset + LENGTH]
    return running

def modal_sum(product, log_rate, residues):
    rate_values = jnp.exp(log_rate)
    places = jnp.arange(TOK_DEV, dtype=jnp.float32)
    lagged = places[:, None] - places[None, :]
    decay = jnp.where(lagged >= 0, jnp.exp(-rate_values[:, :, None, None] * jnp.maximum(lagged, 0.0)), 0.0)
    head_decay = jnp.exp(-rate_values[:, :, None] * (places + 1.0))
    weights = residues.reshape(POLES, GROUPS, GSIZE)
    blocks = product.reshape(N_CTX, TOK_DEV, GROUPS, GSIZE)

    @jax.checkpoint
    def advance(carried, product_block):
        local_part = jnp.einsum('pgts,sgc->pgtc', decay, product_block, precision=HIGHEST)
        states = local_part + head_decay[..., None] * carried[:, :, None, :]
        summed = jnp.einsum('pgtc,pgc->tgc', states, weights, precision=HIGHEST)
        return (states[:, :, TOK_DEV - 1, :], summed.reshape(TOK_DEV, D))
    start_state = jnp.zeros((POLES, GROUPS, GSIZE), jnp.float32)
    _, outputs = lax.scan(advance, start_state, blocks)
    return outputs.reshape(LENGTH, D)

def forward_one(seq_feats, conv_weight, log_rate, residues, skip_weight, norm_gain):
    filtered = short_filter(seq_feats, conv_weight)
    query_rows = filtered[:, 0]
    key_rows = filtered[:, 1]
    value_rows = filtered[:, 2]
    product = key_rows * value_rows
    gated_rows = query_rows * (modal_sum(product, log_rate, residues) + skip_weight * product)
    inv_rms = lax.rsqrt(lax.optimization_barrier(jnp.mean(gated_rows * gated_rows, axis=1, keepdims=True)) + EPSILON)
    return norm_gain * gated_rows * inv_rms

def reference(features, conv_weight, log_rate, residues, skip_weight, norm_gain, cotangent):

    def one_sequence(members):
        seq_feats, seed_grad = members
        result, pullback = jax.vjp(forward_one, seq_feats.astype(jnp.float32), conv_weight, log_rate, residues, skip_weight, norm_gain)
        grads_all = pullback(seed_grad.astype(jnp.float32))
        return (result.astype(jnp.bfloat16), grads_all[0].astype(jnp.bfloat16), grads_all[1], grads_all[2], grads_all[3], grads_all[4], grads_all[5])
    mapped = lax.map(one_sequence, (features, cotangent))
    return (mapped[0], mapped[1], lax.optimization_barrier(jnp.sum(mapped[2], axis=0)), lax.optimization_barrier(jnp.sum(mapped[3], axis=0)), lax.optimization_barrier(jnp.sum(mapped[4], axis=0)), lax.optimization_barrier(jnp.sum(mapped[5], axis=0)), lax.optimization_barrier(jnp.sum(mapped[6], axis=0)))
```

```python
import functools
import jax
import jax.numpy as jnp
from jax import lax
from jax.experimental import pallas as pl
from jax.experimental.pallas import tpu as pltpu
from jax.sharding import PartitionSpec as P

D = 4096
EPSILON = 1e-06
HIGHEST = lax.Precision.HIGHEST
F32 = jnp.float32
BF16 = jnp.bfloat16
L = 128
GS = 128
POLES = 8
TAPS = 7
PAD = 8
GB = 2
ROWS = 32


def params(mib):
    return pltpu.CompilerParams(vmem_limit_bytes=mib * 1024 * 1024)


def iota(shape, dim):
    return lax.broadcasted_iota(jnp.int32, shape, dim)


def ones_tri(lower):
    row = iota((L, 2 * L), 0)
    col = iota((L, 2 * L), 1) % L
    keep = col <= row if lower else col >= row
    return jnp.where(keep, 1.0, 0.0).astype(BF16)


def split(x):
    high = x.astype(BF16)
    low = (x - high.astype(F32)).astype(BF16)
    return jnp.concatenate([high, low], axis=0)


def tri_dot(tri, xs):
    return jnp.dot(tri, jnp.concatenate([split(x) for x in xs], axis=1), preferred_element_type=F32)


def contract_rows(a, b):
    return lax.dot_general(a, b, (((0,), (0,)), ((), ())), precision=HIGHEST, preferred_element_type=F32)


def rowsum(x):
    return jnp.sum(x, axis=0, keepdims=True)


def fill_ext(ext, feat, halo, cs):
    for j in range(3):
        ext[j, 0:PAD, :] = halo[j, :, cs].astype(F32)
        ext[j, PAD : PAD + L, :] = feat[j, :, cs].astype(F32)


def forward_kernel(rate, feat, halo, taps, weight, skip, q_o, k_o, v_o, bl_o, s_o, e_o, ext):
    first = pl.program_id(0) * GB
    tri = ones_tri(True)
    place = iota((L, GS), 0).astype(F32)
    for gi in range(GB):
        cs = slice(gi * GS, (gi + 1) * GS)
        fill_ext(ext, feat, halo, cs)
        rows = []
        for j in range(3):
            acc = taps[j, 0:1, cs] * ext[j, PAD : PAD + L, :]
            for k in range(1, TAPS):
                acc = acc + taps[j, k : k + 1, cs] * ext[j, pl.ds(PAD - k, L), :]
            rows.append(acc)
        q, key, value = rows
        q_o[:, cs] = q
        k_o[:, cs] = key
        v_o[:, cs] = value
        prod = key * value
        modal = skip[0:1, cs] * prod
        for p in range(0, POLES, 2):
            rates = [rate[p + i, first + gi] for i in range(2)]
            both = tri_dot(tri, [jnp.exp(place * r) * prod for r in rates])
            for i, r in enumerate(rates):
                state = jnp.exp(place * (-r)) * both[:, i * GS : (i + 1) * GS]
                s_o[p + i, :, cs] = state
                e_o[gi, p + i : p + i + 1, :] = state[L - 1 : L, :]
                modal = modal + weight[p + i : p + i + 1, cs] * state
        bl_o[:, cs] = modal


def scan_kernel(back, rate, where, rows, out):
    me = where[0]
    group = me // 4
    pole = 2 * (me % 4)
    low, high = rate[pole, group], rate[pole + 1, group]
    row, col = iota((L, L), 0), iota((L, L), 1)
    lag = col // 2 - row // 2 - 1 if back else row // 2 - col // 2 - 1
    keep = (lag >= 0) & (row % 2 == col % 2)
    own = jnp.where(row % 2 == 0, low, high)
    decay = jnp.where(keep, jnp.exp(-(own * L) * jnp.maximum(lag, 0).astype(F32)), 0.0)
    out[...] = jnp.dot(decay, rows[...], precision=HIGHEST, preferred_element_type=F32)


def branch_kernel(q, bl, cot, gain, state_in, head, weight, br_o, stats_o, acc):
    step = pl.program_id(0)

    @pl.when(step == 0)
    def _():
        acc[...] = jnp.zeros_like(acc)

    for gi in range(GB):
        cs = slice(gi * GS, (gi + 1) * GS)
        branch = bl[:, cs] + contract_rows(head[gi], weight[:, cs] * state_in[gi])
        br_o[:, cs] = branch
        gated = q[:, cs] * branch
        acc[0] += gated * gated
        acc[1] += (gain[0:1, cs] * cot[:, cs].astype(F32)) * gated

    @pl.when(step == pl.num_programs(0) - 1)
    def _():
        row = iota((8, L), 0)
        squares = rowsum(acc[0].T)
        slopes = rowsum(acc[1].T)
        stats_o[...] = jnp.where(row == 0, squares, jnp.where(row == 1, slopes, 0.0))


def down(row):
    return jnp.broadcast_to(row, (L, L)).T


def gate_kernel(stats, q, br, cot, gain, k, v, head, out_o, g_o, dq_o, back_o, gain_o, skip_o):
    inv_row = lax.rsqrt(stats[0:1, :] / D + EPSILON)
    inv = down(inv_row)
    pull = down(stats[1:2, :] * inv_row * inv_row * inv_row / D)
    for gi in range(GB):
        cs = slice(gi * GS, (gi + 1) * GS)
        query = q[:, cs]
        branch = br[:, cs]
        grad = cot[:, cs].astype(F32)
        gated = query * branch
        normed = gated * inv
        out_o[:, cs] = (gain[0:1, cs] * normed).astype(BF16)
        gain_o[0:1, cs] = rowsum(grad * normed)
        dgated = (gain[0:1, cs] * grad) * inv - gated * pull
        dq_o[:, cs] = dgated * branch
        dbranch = dgated * query
        g_o[:, cs] = dbranch
        skip_o[0:1, cs] = rowsum(dbranch * (k[:, cs] * v[:, cs]))
        back_o[gi] = jnp.dot(head[gi], dbranch, precision=HIGHEST, preferred_element_type=F32)


def adjoint_kernel(
    rate, g, dq, k, v, states, weight, skip, state_in, back, heads, tails, feat, halo,
    dpl_o, res_o, loc_o, mix_o, cq_o, ext,
):
    first = pl.program_id(0) * GB
    tri = ones_tri(False)
    place = iota((L, GS), 0).astype(F32)
    centre = place - (L - 1) / 2
    for gi in range(GB):
        cs = slice(gi * GS, (gi + 1) * GS)
        dbranch = g[:, cs]
        prod = k[:, cs] * v[:, cs]
        total = skip[0:1, cs] * dbranch
        far_grad = centre * dbranch
        far_prod = centre * prod
        own_in = state_in[gi]
        residue = own_in * back[gi]
        heavy = jnp.dot(heads[gi], dbranch, precision=HIGHEST, preferred_element_type=F32)
        deep = jnp.dot(tails[gi], prod, precision=HIGHEST, preferred_element_type=F32)
        for p in range(0, POLES, 2):
            rates = [rate[p + i, first + gi] for i in range(2)]
            both = tri_dot(tri, [jnp.exp(place * (-r)) * dbranch for r in rates])
            for i, r in enumerate(rates):
                at = slice(p + i, p + i + 1)
                adjoint = jnp.exp(place * r) * both[:, i * GS : (i + 1) * GS]
                total = total + weight[at, cs] * adjoint
                res_o[at, cs] = residue[at, :] + rowsum(prod * adjoint)
                loc_o[at, cs] = rowsum(far_grad * states[p + i, :, cs] - far_prod * adjoint)
        dpl_o[:, cs] = total
        lane_rate = jnp.zeros((POLES, GS), F32)
        for p in range(POLES):
            lane_rate = jnp.where(iota((POLES, GS), 0) == p, rate[p, first + gi], lane_rate)
        once = jnp.exp(-lane_rate)
        loc_o[:, cs] += once * own_in * heavy
        mix_o[:, cs] = once * (deep + L * jnp.exp(-(L - 1) * lane_rate) * own_in)
        fill_ext_one(ext, feat, halo, cs)
        dquery = dq[:, cs]
        for t in range(TAPS):
            cq_o[t : t + 1, cs] = rowsum(dquery * ext[pl.ds(PAD - t, L), :])


def fill_ext_one(ext, feat, halo, cs):
    ext[0:PAD, :] = halo[0, :, cs].astype(F32)
    ext[PAD : PAD + L, :] = feat[0, :, cs].astype(F32)


def finish_kernel(
    rate, later, dpl, dq, k, v, tails, weight, loc, mix, cq, res, skip, gain, feat, halo, rim, taps,
    grad_o, pack_o, ext, dext,
):
    first = pl.program_id(0) * GB
    lane = iota((POLES, GS), 1)
    sub = iota((POLES, GS), 0)
    ahead = (iota((PAD, GS), 0) + 1).astype(F32)
    for gi in range(GB):
        cs = slice(gi * GS, (gi + 1) * GS)
        coming = later[gi]
        dprod = dpl[:, cs] + contract_rows(tails[gi], weight[:, cs] * coming)
        key, value = k[:, cs], v[:, cs]
        dext[0, 0:L, :] = dq[:, cs]
        dext[1, 0:L, :] = dprod * value
        dext[2, 0:L, :] = dprod * key
        beyond = weight[:, cs] * (coming - rim[4, :, cs])
        next_prod = rim[1, :, cs]
        for p in range(POLES):
            next_prod = next_prod + jnp.exp(ahead * rate[p, first + gi]) * beyond[p : p + 1, :]
        dext[0, L : L + PAD, :] = rim[0, :, cs]
        dext[1, L : L + PAD, :] = next_prod * rim[3, :, cs]
        dext[2, L : L + PAD, :] = next_prod * rim[2, :, cs]
        fill_ext(ext, feat, halo, cs)
        pack_o[gi, 0:TAPS, :] = cq[0:TAPS, cs]
        for j in range(3):
            acc = taps[j, 0:1, cs] * dext[j, 0:L, :]
            for t in range(1, TAPS):
                acc = acc + taps[j, t : t + 1, cs] * dext[j, pl.ds(t, L), :]
            grad_o[j, :, cs] = acc.astype(BF16)
            if j:
                own = dext[j, 0:L, :]
                for t in range(TAPS):
                    at = TAPS * j + t
                    pack_o[gi, at : at + 1, :] = rowsum(own * ext[j, pl.ds(PAD - t, L), :])
        pack_o[gi, 21:29, :] = res[:, cs]
        pack_o[gi, 29:30, :] = skip[0:1, cs]
        pack_o[gi, 30:31, :] = gain[0:1, cs]
        inner = jnp.sum(weight[:, cs] * (loc[:, cs] + coming * mix[:, cs]), axis=1, keepdims=True)
        lane_rate = jnp.zeros((POLES, GS), F32)
        for p in range(POLES):
            lane_rate = jnp.where(sub == p, rate[p, first + gi], lane_rate)
        pack_o[gi, 31:32, :] = rowsum(jnp.where(lane == sub, -lane_rate * inner, 0.0))


def add_kernel(parts, out):
    out[...] = jnp.sum(parts[...], axis=0)


def unpack_kernel(pack, conv_o, rate_o, res_o, skip_o, gain_o):
    groups = pack.shape[0]
    for gi in range(groups):
        cs = slice(gi * GS, (gi + 1) * GS)
        for j in range(3):
            conv_o[j, :, cs] = pack[gi, TAPS * j : TAPS * j + TAPS, :]
        res_o[:, cs] = pack[gi, 21:29, :]
        skip_o[0:1, cs] = pack[gi, 29:30, :]
        gain_o[0:1, cs] = pack[gi, 30:31, :]
        rate_o[gi : gi + 1, :] = pack[gi, 31:32, :]


def smem():
    return pl.BlockSpec(memory_space=pltpu.SMEM)


def cols(*lead):
    return pl.BlockSpec((*lead, GB * GS), lambda i: (0,) * len(lead) + (i,))


def groups_of(rows):
    return pl.BlockSpec((GB, rows, GS), lambda i: (i, 0, 0))


def shape(*dims, dtype=F32):
    return jax.ShapeDtypeStruct(dims, dtype)


def local(features, conv_weight, log_rate, residues, skip_weight, norm_gain, cotangent):
    feat = features[0].transpose(1, 0, 2)
    taps = conv_weight.transpose(1, 0, 2)
    cot = cotangent[0]
    channels = feat.shape[2]
    groups = log_rate.shape[1]
    count = lax.axis_size("ctx")
    steps = groups // GB
    skip = skip_weight[None]
    gain = norm_gain[None]
    where = lax.axis_index("ctx").astype(jnp.int32)[None]

    halo = lax.ppermute(feat[:, L - PAD :], "ctx", [(i, i + 1) for i in range(count - 1)])
    rate = jnp.exp(log_rate)
    by_group = rate.T[:, :, None]
    places = jnp.arange(L, dtype=F32)
    head = jnp.exp(-by_group * (places + 1.0))
    heads = (places + 1.0) * jnp.exp(-by_group * places)
    tail = jnp.exp(-by_group * (L - 1.0 - places))
    tails = (L - 1.0 - places) * jnp.exp(-by_group * (L - 2.0 - places))

    query, key, value, base, states, ends = pl.pallas_call(
        forward_kernel,
        grid=(steps,),
        in_specs=[smem(), cols(3, L), cols(3, PAD), cols(3, TAPS), cols(POLES), cols(1)],
        out_specs=[cols(L)] * 4 + [cols(POLES, L), groups_of(POLES)],
        out_shape=[shape(L, channels)] * 4 + [shape(POLES, L, channels), shape(groups, POLES, GS)],
        scratch_shapes=[pltpu.VMEM((3, PAD + L, GS), F32)],
        compiler_params=params(24),
        name="forward_local",
    )(rate, feat, halo, taps, residues, skip)

    def carried(rows, back):
        sent = lax.all_to_all(rows.reshape(count, 2, GS), "ctx", 0, 0)
        summed = pl.pallas_call(
            functools.partial(scan_kernel, back),
            in_specs=[smem(), smem(), pl.BlockSpec((L, GS), lambda: (0, 0))],
            out_specs=pl.BlockSpec((L, GS), lambda: (0, 0)),
            out_shape=shape(L, GS),
            name="carry_back" if back else "carry_on",
        )(rate, where, sent.reshape(L, GS))
        given = lax.all_to_all(summed.reshape(count, 2, GS), "ctx", 0, 0)
        return given.reshape(groups, POLES, GS)

    state_in = carried(ends, False)

    branch, stats = pl.pallas_call(
        branch_kernel,
        grid=(steps,),
        in_specs=[cols(L), cols(L), cols(L), cols(1), groups_of(POLES), groups_of(POLES), cols(POLES)],
        out_specs=[cols(L), pl.BlockSpec((8, L), lambda i: (0, 0))],
        out_shape=[shape(L, channels), shape(8, L)],
        scratch_shapes=[pltpu.VMEM((2, L, GS), F32)],
        compiler_params=params(24),
        name="branch",
    )(query, base, cot, gain, state_in, head, residues)
    stats = lax.psum(stats, "mp")

    block_out, dbranch, dquery, back_in, gain_part, skip_part = pl.pallas_call(
        gate_kernel,
        grid=(steps,),
        in_specs=[pl.BlockSpec((8, L), lambda i: (0, 0))]
        + [cols(L)] * 3
        + [cols(1), cols(L), cols(L), groups_of(POLES)],
        out_specs=[cols(L)] * 3 + [groups_of(POLES), cols(1), cols(1)],
        out_shape=[shape(L, channels, dtype=BF16), shape(L, channels), shape(L, channels)]
        + [shape(groups, POLES, GS), shape(1, channels), shape(1, channels)],
        compiler_params=params(24),
        name="gate",
    )(stats, query, branch, cot, gain, key, value, head)

    dlocal, res_part, loc_part, mix_part, cq_part = pl.pallas_call(
        adjoint_kernel,
        grid=(steps,),
        in_specs=[smem()]
        + [cols(L)] * 4
        + [cols(POLES, L), cols(POLES), cols(1)]
        + [groups_of(POLES)] * 4
        + [cols(3, L), cols(3, PAD)],
        out_specs=[cols(L), cols(POLES), cols(POLES), cols(POLES), cols(TAPS)],
        out_shape=[shape(L, channels)] + [shape(POLES, channels)] * 3 + [shape(TAPS, channels)],
        scratch_shapes=[pltpu.VMEM((PAD + L, GS), F32)],
        compiler_params=params(24),
        cost_estimate=pl.CostEstimate(flops=6_000_000_000, bytes_accessed=16_000_000, transcendentals=4_000_000),
        name="adjoint_local",
    )(rate, dbranch, dquery, key, value, states, residues, skip, state_in, back_in, heads, tails, feat, halo)

    edge = jnp.stack(
        [dquery[:PAD], dlocal[:PAD], key[:PAD], value[:PAD], back_in.transpose(1, 0, 2).reshape(POLES, channels)]
    )
    rim = lax.ppermute(edge, "ctx", [(i + 1, i) for i in range(count - 1)])
    later = carried(back_in, True)

    feature_grad, pack = pl.pallas_call(
        finish_kernel,
        grid=(steps,),
        in_specs=[smem(), groups_of(POLES)]
        + [cols(L)] * 4
        + [groups_of(POLES)]
        + [cols(POLES)] * 3
        + [cols(TAPS), cols(POLES), cols(1), cols(1)]
        + [cols(3, L), cols(3, PAD), cols(5, PAD), cols(3, TAPS)],
        out_specs=[cols(3, L), groups_of(ROWS)],
        out_shape=[shape(3, L, channels, dtype=BF16), shape(groups, ROWS, GS)],
        scratch_shapes=[pltpu.VMEM((3, PAD + L, GS), F32), pltpu.VMEM((3, PAD + L, GS), F32)],
        compiler_params=params(24),
        name="finish",
    )(rate, later, dlocal, dquery, key, value, tail, residues, loc_part, mix_part, cq_part, res_part, skip_part, gain_part, feat, halo, rim, taps)

    share = groups * ROWS // count
    parts = lax.all_to_all(pack.reshape(count, share, GS), "ctx", 0, 0)
    mine = pl.pallas_call(add_kernel, out_shape=shape(share, GS), name="add_parts")(parts)
    mine = lax.psum(mine, "dp")
    totals = lax.all_to_all(jnp.broadcast_to(mine[None], (count, share, GS)), "ctx", 0, 0)
    conv, rate_grad, res, skip_grad, gain_grad = pl.pallas_call(
        unpack_kernel,
        out_shape=[shape(3, TAPS, channels), shape(groups, GS), shape(POLES, channels)] + [shape(1, channels)] * 2,
        name="unpack",
    )(totals.reshape(groups, ROWS, GS))
    return (
        block_out[None],
        feature_grad.transpose(1, 0, 2)[None],
        conv.transpose(1, 0, 2),
        rate_grad[:, :POLES].T,
        res,
        skip_grad[0],
        gain_grad[0],
    )


def solution(mesh):
    in_specs = (
        P("dp", "ctx", None, "mp"),
        P(None, None, "mp"),
        P(None, "mp"),
        P(None, "mp"),
        P("mp"),
        P("mp"),
        P("dp", "ctx", "mp"),
    )
    out_specs = (
        P("dp", "ctx", "mp"),
        P("dp", "ctx", None, "mp"),
        P(None, None, "mp"),
        P(None, "mp"),
        P(None, "mp"),
        P("mp"),
        P("mp"),
    )
    return jax.shard_map(local, mesh=mesh, in_specs=in_specs, out_specs=out_specs, check_vma=False)
```

```python
import functools
import jax
import jax.numpy as jnp
from jax import lax
from jax.experimental import pallas as pl
from jax.experimental.pallas import tpu as pltpu
from jax.sharding import Mesh
from jax.sharding import PartitionSpec as P

D = 4096
EPSILON = 1e-06
HIGHEST = lax.Precision.HIGHEST
F32 = jnp.float32
BF16 = jnp.bfloat16
L = 128
GS = 128
POLES = 8
TAPS = 7
PAD = 8
GB = 2
ROWS = 32
VMEM_MIB = 53
CTX = ("x", "z")
YX = ("y", "x")


def params(mib):
    return pltpu.CompilerParams(vmem_limit_bytes=mib * 1024 * 1024)


def iota(shape, dim):
    return lax.broadcasted_iota(jnp.int32, shape, dim)


def ones_tri(lower):
    row = iota((L, 2 * L), 0)
    col = iota((L, 2 * L), 1) % L
    keep = col <= row if lower else col >= row
    return jnp.where(keep, 1.0, 0.0).astype(BF16)


def split(x):
    high = x.astype(BF16)
    low = (x - high.astype(F32)).astype(BF16)
    return jnp.concatenate([high, low], axis=0)


def tri_dot(tri, xs):
    return jnp.dot(tri, jnp.concatenate([split(x) for x in xs], axis=1), preferred_element_type=F32)


def rowsum(x):
    return jnp.sum(x, axis=0, keepdims=True)


def fill_ext(ext, feat, halo, cs):
    for j in range(3):
        ext[j, 0:PAD, :] = halo[j, :, cs].astype(F32)
        ext[j, PAD : PAD + L, :] = feat[j, :, cs].astype(F32)


def filtered(j, taps, feat, halo, cs, ext):
    ext[j, 0:PAD, :] = halo[j, :, cs].astype(F32)
    ext[j, PAD : PAD + L, :] = feat[j, :, cs].astype(F32)
    acc = taps[j, 0:1, cs] * ext[j, PAD : PAD + L, :]
    for k in range(1, TAPS):
        acc = acc + taps[j, k : k + 1, cs] * ext[j, pl.ds(PAD - k, L), :]
    return acc


def two_parts(table):
    high = table.astype(BF16).astype(F32)
    both = jnp.concatenate([high, table - high], axis=0)
    return jnp.concatenate([both, both], axis=1).astype(BF16)


def weighted_rows(table, x):
    both = jnp.dot(two_parts(table), split(x), preferred_element_type=F32)
    return both[0:POLES, :] + both[POLES : 2 * POLES, :]


def lane_place():
    return iota((POLES, L), 1).astype(F32)


def spread_poles(lane_rate, sign, rows):
    lane = iota((L, 4 * POLES), 1)
    place = iota((L, 4 * POLES), 0).astype(F32)
    steps = place + 1.0 if sign > 0 else L - 1.0 - place
    table = jnp.exp(-steps * lane_rate[:, 0 : 4 * POLES])
    high = table.astype(BF16).astype(F32)
    left = jnp.where((lane // POLES) % 2 == 0, high, table - high).astype(BF16)
    top = rows.astype(BF16).astype(F32)
    low = rows - top
    right = jnp.concatenate([top, top, low, low], axis=0).astype(BF16)
    return jnp.dot(left, right, preferred_element_type=F32)


def ends_kernel(by_pole, feat, halo, taps, k_o, v_o, e_o, edge_o, ext):
    for gi in range(GB):
        cs = slice(gi * GS, (gi + 1) * GS)
        key = filtered(1, taps, feat, halo, cs, ext)
        value = filtered(2, taps, feat, halo, cs, ext)
        k_o[:, cs] = key
        v_o[:, cs] = value
        edge_o[0, :, cs] = key[0:PAD, :]
        edge_o[1, :, cs] = value[0:PAD, :]
        e_o[gi] = weighted_rows(jnp.exp(-by_pole[gi] * (L - 1.0 - lane_place())), key * value)


def states_kernel(rate, feat, halo, taps, k, v, weight, skip, q_o, bl_o, s_o, ext):
    first = pl.program_id(0) * GB
    tri = ones_tri(True)
    place = iota((L, GS), 0).astype(F32)
    for gi in range(GB):
        cs = slice(gi * GS, (gi + 1) * GS)
        q_o[:, cs] = filtered(0, taps, feat, halo, cs, ext)
        prod = k[:, cs] * v[:, cs]
        modal = skip[0:1, cs] * prod
        for p in range(0, POLES, 2):
            rates = [rate[p + i, first + gi] for i in range(2)]
            both = tri_dot(tri, [jnp.exp(place * r) * prod for r in rates])
            for i, r in enumerate(rates):
                state = jnp.exp(place * (-r)) * both[:, i * GS : (i + 1) * GS]
                s_o[p + i, :, cs] = state
                modal = modal + weight[p + i : p + i + 1, cs] * state
        bl_o[:, cs] = modal


def coefs_kernel(by_pole, k, v, feat, halo, c_o, ext):
    for gi in range(GB):
        cs = slice(gi * GS, (gi + 1) * GS)
        fill_ext(ext, feat, halo, cs)
        table = two_parts(jnp.exp(-by_pole[gi] * (L - 1.0 - lane_place())))
        for j, other in ((1, v[:, cs]), (2, k[:, cs])):
            xs = [split(other * ext[j, pl.ds(PAD - t, L), :]) for t in range(TAPS)]
            both = jnp.dot(table, jnp.concatenate(xs, axis=1), preferred_element_type=F32)
            both = both[0:POLES, :] + both[POLES : 2 * POLES, :]
            for t in range(TAPS):
                at = POLES * (TAPS * (j - 1) + t)
                c_o[gi, at : at + POLES, :] = both[:, t * GS : (t + 1) * GS]


def scan_kernel(back, rate, where, rows, out):
    me = where[0]
    group = me // 4
    pole = 2 * (me % 4)
    low, high = rate[pole, group], rate[pole + 1, group]
    row, col = iota((L, L), 0), iota((L, L), 1)
    lag = col // 2 - row // 2 - 1 if back else row // 2 - col // 2 - 1
    keep = (lag >= 0) & (row % 2 == col % 2)
    own = jnp.where(row % 2 == 0, low, high)
    decay = jnp.where(keep, jnp.exp(-(own * L) * jnp.maximum(lag, 0).astype(F32)), 0.0)
    out[...] = jnp.dot(decay, rows[...], precision=HIGHEST, preferred_element_type=F32)


def branch_kernel(q, bl, cot, gain, state_in, by_lane, weight, br_o, stats_o, acc):
    step = pl.program_id(0)

    @pl.when(step == 0)
    def _():
        acc[...] = jnp.zeros_like(acc)

    for gi in range(GB):
        cs = slice(gi * GS, (gi + 1) * GS)
        branch = bl[:, cs] + spread_poles(by_lane[gi], 1, weight[:, cs] * state_in[gi])
        br_o[:, cs] = branch
        gated = q[:, cs] * branch
        acc[0] += gated * gated
        acc[1] += (gain[0:1, cs] * cot[:, cs].astype(F32)) * gated

    @pl.when(step == pl.num_programs(0) - 1)
    def _():
        row = iota((8, L), 0)
        squares = rowsum(acc[0].T)
        slopes = rowsum(acc[1].T)
        stats_o[...] = jnp.where(row == 0, squares, jnp.where(row == 1, slopes, 0.0))


def down(row):
    return jnp.broadcast_to(row, (L, L)).T


def gate_kernel(stats, q, br, cot, gain, by_pole, g_o, back_o, edge_o):
    inv_row = lax.rsqrt(stats[0:1, :] / D + EPSILON)
    inv = down(inv_row)
    pull = down(stats[1:2, :] * inv_row * inv_row * inv_row / D)
    for gi in range(GB):
        cs = slice(gi * GS, (gi + 1) * GS)
        query, branch = q[:, cs], br[:, cs]
        dgated = (gain[0:1, cs] * cot[:, cs].astype(F32)) * inv - (query * branch) * pull
        dbranch = dgated * query
        g_o[:, cs] = dbranch
        back = weighted_rows(jnp.exp(-by_pole[gi] * (lane_place() + 1.0)), dbranch)
        back_o[gi] = back
        edge_o[0, :, cs] = dgated[0:PAD, :] * branch[0:PAD, :]
        edge_o[1, :, cs] = back


def adjoint_kernel(
    rate, by_pole, g, k, v, states, weight, skip, state_in, back, edge,
    dpl_o, res_o, loc_o, mix_o, edge_o,
):
    first = pl.program_id(0) * GB
    tri = ones_tri(False)
    place = iota((L, GS), 0).astype(F32)
    centre = place - (L - 1) / 2
    lane = lane_place()
    for gi in range(GB):
        cs = slice(gi * GS, (gi + 1) * GS)
        dbranch = g[:, cs]
        prod = k[:, cs] * v[:, cs]
        total = skip[0:1, cs] * dbranch
        far_grad = centre * dbranch
        far_prod = centre * prod
        own_in = state_in[gi]
        own_rate = by_pole[gi]
        once = jnp.exp(-own_rate)
        residue = own_in * back[gi]
        heavy = weighted_rows((lane + 1.0) * jnp.exp(-own_rate * lane), dbranch)
        deep = weighted_rows((L - 1.0 - lane) * jnp.exp(-own_rate * (L - 2.0 - lane)), prod)
        mix_o[gi] = once * (deep + L * jnp.exp(-(L - 1) * own_rate) * own_in)
        loc = once * own_in * heavy
        for p in range(0, POLES, 2):
            rates = [rate[p + i, first + gi] for i in range(2)]
            both = tri_dot(tri, [jnp.exp(place * (-r)) * dbranch for r in rates])
            for i, r in enumerate(rates):
                at = slice(p + i, p + i + 1)
                adjoint = jnp.exp(place * r) * both[:, i * GS : (i + 1) * GS]
                total = total + weight[at, cs] * adjoint
                res_o[gi, at, :] = residue[at, :] + rowsum(prod * adjoint)
                loc_o[gi, at, :] = loc[at, :] + rowsum(far_grad * states[p + i, :, cs] - far_prod * adjoint)
        dpl_o[:, cs] = total
        edge_o[0, :, cs] = edge[0, :, cs]
        edge_o[1, :, cs] = total[0:PAD, :]
        edge_o[2, :, cs] = edge[1, :, cs]


def outs_kernel(
    stats, q, br, cot, gain, k, v, g, dpl, res, feat, halo, out_o, dq_o, pack_o, ext,
):
    inv_row = lax.rsqrt(stats[0:1, :] / D + EPSILON)
    inv = down(inv_row)
    pull = down(stats[1:2, :] * inv_row * inv_row * inv_row / D)
    for gi in range(GB):
        cs = slice(gi * GS, (gi + 1) * GS)
        fill_ext(ext, feat, halo, cs)
        query, branch, key, value = q[:, cs], br[:, cs], k[:, cs], v[:, cs]
        grad = cot[:, cs].astype(F32)
        gated = query * branch
        normed = gated * inv
        out_o[:, cs] = (gain[0:1, cs] * normed).astype(BF16)
        dquery = ((gain[0:1, cs] * grad) * inv - gated * pull) * branch
        dq_o[:, cs] = dquery
        local_prod = dpl[:, cs]
        for j, own in enumerate((dquery, local_prod * value, local_prod * key)):
            for t in range(TAPS):
                at = TAPS * j + t
                pack_o[gi, at : at + 1, :] = rowsum(own * ext[j, pl.ds(PAD - t, L), :])
        pack_o[gi, 21:29, :] = res[gi]
        pack_o[gi, 29:30, :] = rowsum(g[:, cs] * (key * value))
        pack_o[gi, 30:31, :] = rowsum(grad * normed)
        pack_o[gi, 31:32, :] = jnp.zeros((1, GS), F32)


def sums_kernel(later, by_pole, weight, loc, mix, coefs, pack, pack_o):
    lane, sub = iota((POLES, GS), 1), iota((POLES, GS), 0)
    for gi in range(GB):
        cs = slice(gi * GS, (gi + 1) * GS)
        coming = later[gi]
        scaled = weight[:, cs] * coming
        pack_o[gi] = pack[gi]
        for i in range(2 * TAPS):
            at = TAPS + i
            more = rowsum(scaled * coefs[gi, POLES * i : POLES * (i + 1), :])
            pack_o[gi, at : at + 1, :] = pack[gi, at : at + 1, :] + more
        inner = jnp.sum(weight[:, cs] * (loc[gi] + coming * mix[gi]), axis=1, keepdims=True)
        pack_o[gi, 31:32, :] = rowsum(jnp.where(lane == sub, -by_pole[gi] * inner, 0.0))


def finish_kernel(rate, later, by_lane, dpl, dq, k, v, weight, rim, near, taps, grad_o, dext):
    first = pl.program_id(0) * GB
    ahead = (iota((PAD, GS), 0) + 1).astype(F32)
    for gi in range(GB):
        cs = slice(gi * GS, (gi + 1) * GS)
        coming = later[gi]
        dprod = dpl[:, cs] + spread_poles(by_lane[gi], -1, weight[:, cs] * coming)
        dext[0, 0:L, :] = dq[:, cs]
        dext[1, 0:L, :] = dprod * v[:, cs]
        dext[2, 0:L, :] = dprod * k[:, cs]
        beyond = weight[:, cs] * (coming - rim[2, :, cs])
        next_prod = rim[1, :, cs]
        for p in range(POLES):
            next_prod = next_prod + jnp.exp(ahead * rate[p, first + gi]) * beyond[p : p + 1, :]
        dext[0, L : L + PAD, :] = rim[0, :, cs]
        dext[1, L : L + PAD, :] = next_prod * near[1, :, cs]
        dext[2, L : L + PAD, :] = next_prod * near[0, :, cs]
        for j in range(3):
            acc = taps[j, 0:1, cs] * dext[j, 0:L, :]
            for t in range(1, TAPS):
                acc = acc + taps[j, t : t + 1, cs] * dext[j, pl.ds(t, L), :]
            grad_o[j, :, cs] = acc.astype(BF16)


def unpack_kernel(pack, conv_o, rate_o, res_o, skip_o, gain_o):
    groups = pack.shape[0]
    for gi in range(groups):
        cs = slice(gi * GS, (gi + 1) * GS)
        for j in range(3):
            conv_o[j, :, cs] = pack[gi, TAPS * j : TAPS * j + TAPS, :]
        res_o[:, cs] = pack[gi, 21:29, :]
        skip_o[0:1, cs] = pack[gi, 29:30, :]
        gain_o[0:1, cs] = pack[gi, 30:31, :]
        rate_o[gi : gi + 1, :] = pack[gi, 31:32, :]


def smem():
    return pl.BlockSpec(memory_space=pltpu.SMEM)


def cols(*lead):
    return pl.BlockSpec((*lead, GB * GS), lambda i: (0,) * len(lead) + (i,))


def groups_of(rows):
    return pl.BlockSpec((GB, rows, GS), lambda i: (i, 0, 0))


def shape(*dims, dtype=F32):
    return jax.ShapeDtypeStruct(dims, dtype)


def shifted(value, step):
    pairs = [(i, i + step) for i in range(64) if 0 <= i + step < 64]
    return lax.ppermute(value, CTX, pairs)


def local(features, conv_weight, log_rate, residues, skip_weight, norm_gain, cotangent):
    feat = features[0].transpose(1, 0, 2)
    taps = conv_weight.transpose(1, 0, 2)
    cot = cotangent[0]
    channels = feat.shape[2]
    groups = log_rate.shape[1]
    count = lax.axis_size(CTX)
    skip = skip_weight[None]
    gain = norm_gain[None]
    where = lax.axis_index(CTX).astype(jnp.int32)[None]

    def call(kernel, ins, outs, args, scratch=(), flops=0, moved=0, special=0):
        return pl.pallas_call(
            kernel,
            grid=(groups // GB,),
            in_specs=ins,
            out_specs=[o[0] for o in outs],
            out_shape=[o[1] for o in outs],
            scratch_shapes=[pltpu.VMEM(d, F32) for d in scratch],
            compiler_params=params(VMEM_MIB),
            cost_estimate=pl.CostEstimate(flops=flops, bytes_accessed=moved, transcendentals=special),
            name=kernel.__name__,
        )(*args)

    wide = (cols(L), shape(L, channels))
    per_pole = (groups_of(POLES), shape(groups, POLES, GS))
    ext3 = (3, PAD + L, GS)

    halo = shifted(feat[:, L - PAD :], 1)
    rate = jnp.exp(log_rate)
    by_pole = jnp.broadcast_to(rate.T[:, :, None], (groups, POLES, GS))
    by_lane = jnp.tile(rate.T, (1, GS // POLES))[:, None, :]
    poles, lanes = groups_of(POLES), groups_of(1)

    key, value, ends, edge = call(
        ends_kernel,
        [poles, cols(3, L), cols(3, PAD), cols(3, TAPS)],
        [wide, wide, per_pole, (cols(2, PAD), shape(2, PAD, channels))],
        (by_pole, feat, halo, taps),
        [ext3],
    )
    near = shifted(edge, -1)

    def carried(rows, back):
        sent = lax.all_to_all(rows.reshape(count, 2, GS), CTX, 0, 0)
        summed = pl.pallas_call(
            functools.partial(scan_kernel, back),
            in_specs=[smem(), smem(), pl.BlockSpec((L, GS), lambda: (0, 0))],
            out_specs=pl.BlockSpec((L, GS), lambda: (0, 0)),
            out_shape=shape(L, GS),
            compiler_params=params(16),
            name="carry_back" if back else "carry_on",
        )(rate, where, sent.reshape(L, GS))
        given = lax.all_to_all(summed.reshape(count, 2, GS), CTX, 0, 0)
        return given.reshape(groups, POLES, GS)

    state_in = carried(ends, False)

    query, base, states = call(
        states_kernel,
        [smem(), cols(3, L), cols(3, PAD), cols(3, TAPS), cols(L), cols(L), cols(POLES), cols(1)],
        [wide, wide, (cols(POLES, L), shape(POLES, L, channels))],
        (rate, feat, halo, taps, key, value, residues, skip),
        [ext3],
        flops=4_000_000_000,
        moved=14_000_000,
        special=4_000_000,
    )
    coefs = call(
        coefs_kernel,
        [poles, cols(L), cols(L), cols(3, L), cols(3, PAD)],
        [(groups_of(2 * TAPS * POLES), shape(groups, 2 * TAPS * POLES, GS))],
        (by_pole, key, value, feat, halo),
        [ext3],
        flops=4_000_000_000,
        moved=4_000_000,
    )[0]

    branch, stats = call(
        branch_kernel,
        [cols(L), cols(L), cols(L), cols(1), poles, lanes, cols(POLES)],
        [wide, (pl.BlockSpec((8, L), lambda i: (0, 0)), shape(8, L))],
        (query, base, cot, gain, state_in, by_lane, residues),
        [(2, L, GS)],
    )
    stats = lax.psum(stats, "c")
    small = pl.BlockSpec((8, L), lambda i: (0, 0))

    dbranch, back_in, edge = call(
        gate_kernel,
        [small] + [cols(L)] * 3 + [cols(1), poles],
        [wide, per_pole, (cols(2, PAD), shape(2, PAD, channels))],
        (stats, query, branch, cot, gain, by_pole),
    )
    later = carried(back_in, True)

    dlocal, res_part, loc_part, mix_part, edge = call(
        adjoint_kernel,
        [smem(), poles] + [cols(L)] * 3 + [cols(POLES, L), cols(POLES), cols(1), poles, poles, cols(2, PAD)],
        [wide, per_pole, per_pole, per_pole, (cols(3, PAD), shape(3, PAD, channels))],
        (rate, by_pole, dbranch, key, value, states, residues, skip, state_in, back_in, edge),
        flops=6_000_000_000,
        moved=16_000_000,
        special=4_000_000,
    )
    rim = shifted(edge, -1)

    block_out, dquery, pack = call(
        outs_kernel,
        [small] + [cols(L)] * 3 + [cols(1)] + [cols(L)] * 4 + [poles, cols(3, L), cols(3, PAD)],
        [(cols(L), shape(L, channels, dtype=BF16)), wide, (groups_of(ROWS), shape(groups, ROWS, GS))],
        (stats, query, branch, cot, gain, key, value, dbranch, dlocal, res_part, feat, halo),
        [ext3],
        flops=1_000_000_000,
        moved=10_000_000,
    )
    pack = call(
        sums_kernel,
        [poles, poles, cols(POLES), poles, poles, groups_of(2 * TAPS * POLES), groups_of(ROWS)],
        [(groups_of(ROWS), shape(groups, ROWS, GS))],
        (later, by_pole, residues, loc_part, mix_part, coefs, pack),
    )[0]
    feature_grad = call(
        finish_kernel,
        [smem(), poles, lanes] + [cols(L)] * 4 + [cols(POLES), cols(3, PAD), cols(2, PAD), cols(3, TAPS)],
        [(cols(3, L), shape(3, L, channels, dtype=BF16))],
        (rate, later, by_lane, dlocal, dquery, key, value, residues, rim, near, taps),
        [ext3],
        flops=1_000_000_000,
        moved=10_000_000,
    )[0]

    parts = lax.all_to_all(pack, YX, 0, 0)
    mine = lax.psum(jnp.sum(parts, axis=0), "z")
    totals = lax.all_to_all(jnp.broadcast_to(mine[None], (groups, ROWS, GS)), YX, 0, 0)
    conv, rate_grad, res, skip_grad, gain_grad = pl.pallas_call(
        unpack_kernel,
        out_shape=[shape(3, TAPS, channels), shape(groups, GS), shape(POLES, channels)] + [shape(1, channels)] * 2,
        compiler_params=params(16),
        name="unpack",
    )(totals)
    return (
        block_out[None],
        feature_grad.transpose(1, 0, 2)[None],
        conv.transpose(1, 0, 2),
        rate_grad[:, :POLES].T,
        res,
        skip_grad[0],
        gain_grad[0],
    )


def solution(mesh):
    split_mesh = Mesh(mesh.devices.reshape(4, 4, 16, 2), ("y", "x", "z", "c"))
    in_specs = (
        P("y", CTX, None, "c"),
        P(None, None, "c"),
        P(None, "c"),
        P(None, "c"),
        P("c"),
        P("c"),
        P("y", CTX, "c"),
    )
    out_specs = (
        P("y", CTX, "c"),
        P("y", CTX, None, "c"),
        P(None, None, "c"),
        P(None, "c"),
        P(None, "c"),
        P("c"),
        P("c"),
    )
    return jax.shard_map(local, mesh=split_mesh, in_specs=in_specs, out_specs=out_specs, check_vma=False)
```

```python
import functools
import jax
import jax.numpy as jnp
from jax import lax
from jax.experimental import pallas as pl
from jax.experimental.pallas import tpu as pltpu
from jax.sharding import Mesh
from jax.sharding import PartitionSpec as P

D = 4096
EPSILON = 1e-06
HIGHEST = lax.Precision.HIGHEST
F32 = jnp.float32
BF16 = jnp.bfloat16
L = 128
GS = 128
POLES = 8
TAPS = 7
PAD = 8
GROUPS_HERE = 16
PARTS = 4
HELD = ("smem", "vmem", "order")
C, G, W, S, V, O = "cols", "groups", "whole", "smem", "vmem", "order"
ROWS = 32
VMEM_MIB = 53
CTX = ("x", "z")


def window(ref, kind, part):
    if kind == "cols":
        span = ref.shape[-1] // PARTS
        at = pl.ds(pl.multiple_of(part * span, span), span)
        return ref.at[(slice(None),) * (len(ref.shape) - 1) + (at,)]
    if kind == "groups":
        span = ref.shape[0] // PARTS
        return ref.at[pl.ds(part * span, span)]
    return ref


def streamed(setup, kinds_in, kinds_out, *refs):
    ins, outs = refs[: len(kinds_in)], refs[len(kinds_in) : len(kinds_in) + len(kinds_out)]
    rest = list(refs[len(kinds_in) + len(kinds_out) :])
    sems, scratch = rest[0], rest[1:]
    moved = [k for k in kinds_in if k not in HELD]
    in_bufs = scratch[: len(moved)]
    out_bufs = scratch[len(moved) : len(moved) + len(kinds_out)]
    extra = scratch[len(moved) + len(kinds_out) :]
    sources = [r for r, k in zip(ins, kinds_in) if k not in HELD]

    def fetch(n, part):
        src, dst = window(sources[n], moved[n], part), window(in_bufs[n], moved[n], part)
        return pltpu.make_async_copy(src, dst, sems.at[n, part])

    def store(n, part):
        src, dst = window(out_bufs[n], kinds_out[n], part), window(outs[n], kinds_out[n], part)
        return pltpu.make_async_copy(src, dst, sems.at[len(moved) + n, part])

    for n, kind in enumerate(moved):
        if kind == "whole":
            fetch(n, 0).start()

    def begin(part, carry):
        for n, kind in enumerate(moved):
            if kind != "whole":
                fetch(n, part).start()
        return carry

    lax.fori_loop(0, PARTS, begin, 0)
    for n, kind in enumerate(moved):
        if kind == "whole":
            fetch(n, 0).wait()
    buffers = iter(in_bufs)
    views = [r if k in HELD else next(buffers) for r, k in zip(ins, kinds_in)]
    body, last = setup(*[v for v, k in zip(views, kinds_in) if k != "order"], *out_bufs, *extra)
    per_part = GROUPS_HERE // PARTS

    def step(part, carry):
        for n, kind in enumerate(moved):
            if kind != "whole":
                fetch(n, part).wait()
        for i in range(per_part):
            gi = part * per_part + i
            body(gi, pl.ds(pl.multiple_of(gi * GS, GS), GS))
        for n, kind in enumerate(kinds_out):
            if kind != "whole":
                store(n, part).start()
        return carry

    lax.fori_loop(0, PARTS, step, 0)
    if last is not None:
        last()
    for n, kind in enumerate(kinds_out):
        if kind == "whole":
            store(n, 0).start()

    def end(part, carry):
        for n, kind in enumerate(kinds_out):
            if kind != "whole":
                store(n, part).wait()
        return carry

    lax.fori_loop(0, PARTS, end, 0)
    for n, kind in enumerate(kinds_out):
        if kind == "whole":
            store(n, 0).wait()


def params(mib):
    return pltpu.CompilerParams(vmem_limit_bytes=mib * 1024 * 1024)


def iota(shape, dim):
    return lax.broadcasted_iota(jnp.int32, shape, dim)


def ones_tri(lower):
    row = iota((L, 2 * L), 0)
    col = iota((L, 2 * L), 1) % L
    keep = col <= row if lower else col >= row
    return jnp.where(keep, 1.0, 0.0).astype(BF16)


def split(x):
    high = x.astype(BF16)
    low = (x - high.astype(F32)).astype(BF16)
    return jnp.concatenate([high, low], axis=0)


def tri_dot(tri, xs):
    return jnp.dot(tri, jnp.concatenate([split(x) for x in xs], axis=1), preferred_element_type=F32)


def rowsum(x):
    return jnp.sum(x, axis=0, keepdims=True)


def fill_ext(ext, feat, halo, cs):
    for j in range(3):
        ext[j, 0:PAD, :] = halo[j, :, cs].astype(F32)
        ext[j, PAD : PAD + L, :] = feat[j, :, cs].astype(F32)


def filtered(j, taps, feat, halo, cs, ext):
    ext[j, 0:PAD, :] = halo[j, :, cs].astype(F32)
    ext[j, PAD : PAD + L, :] = feat[j, :, cs].astype(F32)
    acc = taps[j, 0:1, cs] * ext[j, PAD : PAD + L, :]
    for k in range(1, TAPS):
        acc = acc + taps[j, k : k + 1, cs] * ext[j, pl.ds(PAD - k, L), :]
    return acc


def two_parts(table):
    high = table.astype(BF16).astype(F32)
    both = jnp.concatenate([high, table - high], axis=0)
    return jnp.concatenate([both, both], axis=1).astype(BF16)


def weighted_rows(table, x):
    both = jnp.dot(two_parts(table), split(x), preferred_element_type=F32)
    return both[0:POLES, :] + both[POLES : 2 * POLES, :]


def lane_place():
    return iota((POLES, L), 1).astype(F32)


def spread_poles(lane_rate, sign, rows):
    lane = iota((L, 4 * POLES), 1)
    place = iota((L, 4 * POLES), 0).astype(F32)
    steps = place + 1.0 if sign > 0 else L - 1.0 - place
    table = jnp.exp(-steps * lane_rate[:, 0 : 4 * POLES])
    high = table.astype(BF16).astype(F32)
    left = jnp.where((lane // POLES) % 2 == 0, high, table - high).astype(BF16)
    top = rows.astype(BF16).astype(F32)
    low = rows - top
    right = jnp.concatenate([top, top, low, low], axis=0).astype(BF16)
    return jnp.dot(left, right, preferred_element_type=F32)


def ends_kernel(by_pole, feat, halo, taps, k_o, v_o, e_o, edge_o, ext):
    def body(gi, cs):
        key = filtered(1, taps, feat, halo, cs, ext)
        value = filtered(2, taps, feat, halo, cs, ext)
        k_o[:, cs] = key
        v_o[:, cs] = value
        edge_o[0, :, cs] = key[0:PAD, :]
        edge_o[1, :, cs] = value[0:PAD, :]
        e_o[gi] = weighted_rows(jnp.exp(-by_pole[gi] * (L - 1.0 - lane_place())), key * value)

    return body, None


def states_kernel(rate, feat, halo, taps, k, v, weight, skip, q_o, bl_o, s_o, ext):
    tri = ones_tri(True)
    place = iota((L, GS), 0).astype(F32)
    def body(gi, cs):
        q_o[:, cs] = filtered(0, taps, feat, halo, cs, ext)
        prod = k[:, cs] * v[:, cs]
        modal = skip[0:1, cs] * prod
        for p in range(0, POLES, 2):
            rates = [rate[p + i, gi] for i in range(2)]
            both = tri_dot(tri, [jnp.exp(place * r) * prod for r in rates])
            for i, r in enumerate(rates):
                state = jnp.exp(place * (-r)) * both[:, i * GS : (i + 1) * GS]
                s_o[p + i, :, cs] = state
                modal = modal + weight[p + i : p + i + 1, cs] * state
        bl_o[:, cs] = modal

    return body, None


def coefs_kernel(by_pole, k, v, feat, halo, c_o, ext):
    def body(gi, cs):
        fill_ext(ext, feat, halo, cs)
        table = two_parts(jnp.exp(-by_pole[gi] * (L - 1.0 - lane_place())))
        for j, other in ((1, v[:, cs]), (2, k[:, cs])):
            xs = [split(other * ext[j, pl.ds(PAD - t, L), :]) for t in range(TAPS)]
            both = jnp.dot(table, jnp.concatenate(xs, axis=1), preferred_element_type=F32)
            both = both[0:POLES, :] + both[POLES : 2 * POLES, :]
            for t in range(TAPS):
                at = POLES * (TAPS * (j - 1) + t)
                c_o[gi, at : at + POLES, :] = both[:, t * GS : (t + 1) * GS]

    return body, None


def scan_kernel(back, rate, where, rows, *refs):
    me = where[0]
    group = me // 4
    pole = 2 * (me % 4)
    low, high = rate[pole, group], rate[pole + 1, group]
    row, col = iota((L, L), 0), iota((L, L), 1)
    lag = col // 2 - row // 2 - 1 if back else row // 2 - col // 2 - 1
    keep = (lag >= 0) & (row % 2 == col % 2)
    own = jnp.where(row % 2 == 0, low, high)
    decay = jnp.where(keep, jnp.exp(-(own * L) * jnp.maximum(lag, 0).astype(F32)), 0.0)
    refs[-1][...] = jnp.dot(decay, rows[...], precision=HIGHEST, preferred_element_type=F32)


def branch_kernel(q, bl, cot, gain, state_in, by_lane, weight, br_o, stats_o, acc):
    acc[...] = jnp.zeros_like(acc)

    def body(gi, cs):
        branch = bl[:, cs] + spread_poles(by_lane[gi], 1, weight[:, cs] * state_in[gi])
        br_o[:, cs] = branch
        gated = q[:, cs] * branch
        acc[0] += gated * gated
        acc[1] += (gain[0:1, cs] * cot[:, cs].astype(F32)) * gated

    def last():
        row = iota((8, L), 0)
        squares = rowsum(acc[0].T)
        slopes = rowsum(acc[1].T)
        stats_o[...] = jnp.where(row == 0, squares, jnp.where(row == 1, slopes, 0.0))

    return body, last


def down(row):
    return jnp.broadcast_to(row, (L, L)).T


def gate_kernel(stats, q, br, cot, gain, by_pole, g_o, back_o, edge_o):
    inv_row = lax.rsqrt(stats[0:1, :] / D + EPSILON)
    inv = down(inv_row)
    pull = down(stats[1:2, :] * inv_row * inv_row * inv_row / D)
    def body(gi, cs):
        query, branch = q[:, cs], br[:, cs]
        dgated = (gain[0:1, cs] * cot[:, cs].astype(F32)) * inv - (query * branch) * pull
        dbranch = dgated * query
        g_o[:, cs] = dbranch
        back = weighted_rows(jnp.exp(-by_pole[gi] * (lane_place() + 1.0)), dbranch)
        back_o[gi] = back
        edge_o[0, :, cs] = dgated[0:PAD, :] * branch[0:PAD, :]
        edge_o[1, :, cs] = back

    return body, None


def adjoint_kernel(
    rate, by_pole, g, k, v, states, weight, skip, state_in, back, edge,
    dpl_o, res_o, loc_o, mix_o, edge_o,
):
    tri = ones_tri(False)
    place = iota((L, GS), 0).astype(F32)
    centre = place - (L - 1) / 2
    lane = lane_place()
    def body(gi, cs):
        dbranch = g[:, cs]
        prod = k[:, cs] * v[:, cs]
        total = skip[0:1, cs] * dbranch
        far_grad = centre * dbranch
        far_prod = centre * prod
        own_in = state_in[gi]
        own_rate = by_pole[gi]
        once = jnp.exp(-own_rate)
        residue = own_in * back[gi]
        heavy = weighted_rows((lane + 1.0) * jnp.exp(-own_rate * lane), dbranch)
        deep = weighted_rows((L - 1.0 - lane) * jnp.exp(-own_rate * (L - 2.0 - lane)), prod)
        mix_o[gi] = once * (deep + L * jnp.exp(-(L - 1) * own_rate) * own_in)
        loc = once * own_in * heavy
        for p in range(0, POLES, 2):
            rates = [rate[p + i, gi] for i in range(2)]
            both = tri_dot(tri, [jnp.exp(place * (-r)) * dbranch for r in rates])
            for i, r in enumerate(rates):
                at = slice(p + i, p + i + 1)
                adjoint = jnp.exp(place * r) * both[:, i * GS : (i + 1) * GS]
                total = total + weight[at, cs] * adjoint
                res_o[gi, at, :] = residue[at, :] + rowsum(prod * adjoint)
                loc_o[gi, at, :] = loc[at, :] + rowsum(far_grad * states[p + i, :, cs] - far_prod * adjoint)
        dpl_o[:, cs] = total
        edge_o[0, :, cs] = edge[0, :, cs]
        edge_o[1, :, cs] = total[0:PAD, :]
        edge_o[2, :, cs] = edge[1, :, cs]

    return body, None


def outs_kernel(
    stats, q, br, cot, gain, k, v, g, dpl, res, feat, halo, out_o, dq_o, pack_o, ext,
):
    inv_row = lax.rsqrt(stats[0:1, :] / D + EPSILON)
    inv = down(inv_row)
    pull = down(stats[1:2, :] * inv_row * inv_row * inv_row / D)
    def body(gi, cs):
        fill_ext(ext, feat, halo, cs)
        query, branch, key, value = q[:, cs], br[:, cs], k[:, cs], v[:, cs]
        grad = cot[:, cs].astype(F32)
        gated = query * branch
        normed = gated * inv
        out_o[:, cs] = (gain[0:1, cs] * normed).astype(BF16)
        dquery = ((gain[0:1, cs] * grad) * inv - gated * pull) * branch
        dq_o[:, cs] = dquery
        local_prod = dpl[:, cs]
        for j, own in enumerate((dquery, local_prod * value, local_prod * key)):
            for t in range(TAPS):
                at = TAPS * j + t
                pack_o[gi, at : at + 1, :] = rowsum(own * ext[j, pl.ds(PAD - t, L), :])
        pack_o[gi, 21:29, :] = res[gi]
        pack_o[gi, 29:30, :] = rowsum(g[:, cs] * (key * value))
        pack_o[gi, 30:31, :] = rowsum(grad * normed)
        pack_o[gi, 31:32, :] = jnp.zeros((1, GS), F32)

    return body, None


def sums_kernel(later, by_pole, weight, loc, mix, coefs, pack, pack_o):
    lane, sub = iota((POLES, GS), 1), iota((POLES, GS), 0)
    def body(gi, cs):
        coming = later[gi]
        scaled = weight[:, cs] * coming
        pack_o[gi] = pack[gi]
        for i in range(2 * TAPS):
            at = TAPS + i
            more = rowsum(scaled * coefs[gi, POLES * i : POLES * (i + 1), :])
            pack_o[gi, at : at + 1, :] = pack[gi, at : at + 1, :] + more
        inner = jnp.sum(weight[:, cs] * (loc[gi] + coming * mix[gi]), axis=1, keepdims=True)
        pack_o[gi, 31:32, :] = rowsum(jnp.where(lane == sub, -by_pole[gi] * inner, 0.0))

    return body, None


def finish_kernel(rate, later, by_lane, dpl, dq, k, v, weight, rim, near, taps, grad_o, dext):
    ahead = (iota((PAD, GS), 0) + 1).astype(F32)
    def body(gi, cs):
        coming = later[gi]
        dprod = dpl[:, cs] + spread_poles(by_lane[gi], -1, weight[:, cs] * coming)
        dext[0, 0:L, :] = dq[:, cs]
        dext[1, 0:L, :] = dprod * v[:, cs]
        dext[2, 0:L, :] = dprod * k[:, cs]
        beyond = weight[:, cs] * (coming - rim[2, :, cs])
        next_prod = rim[1, :, cs]
        for p in range(POLES):
            next_prod = next_prod + jnp.exp(ahead * rate[p, gi]) * beyond[p : p + 1, :]
        dext[0, L : L + PAD, :] = rim[0, :, cs]
        dext[1, L : L + PAD, :] = next_prod * near[1, :, cs]
        dext[2, L : L + PAD, :] = next_prod * near[0, :, cs]
        for j in range(3):
            acc = taps[j, 0:1, cs] * dext[j, 0:L, :]
            for t in range(1, TAPS):
                acc = acc + taps[j, t : t + 1, cs] * dext[j, pl.ds(t, L), :]
            grad_o[j, :, cs] = acc.astype(BF16)

    return body, None


def unpack_kernel(pack, conv_o, rate_o, res_o, skip_o, gain_o):
    groups = pack.shape[0]
    for gi in range(groups):
        cs = slice(gi * GS, (gi + 1) * GS)
        for j in range(3):
            conv_o[j, :, cs] = pack[gi, TAPS * j : TAPS * j + TAPS, :]
        res_o[:, cs] = pack[gi, 21:29, :]
        skip_o[0:1, cs] = pack[gi, 29:30, :]
        gain_o[0:1, cs] = pack[gi, 30:31, :]
        rate_o[gi : gi + 1, :] = pack[gi, 31:32, :]


def smem():
    return pl.BlockSpec(memory_space=pltpu.SMEM)


def vmem():
    return pl.BlockSpec(memory_space=pltpu.VMEM)


def shape(*dims, dtype=F32):
    return jax.ShapeDtypeStruct(dims, dtype)


ends_kernel.kinds = ((W, C, V, C,), (C, C, G, C,))
states_kernel.kinds = ((S, C, V, C, C, C, C, C,), (C, C, C,))
coefs_kernel.kinds = ((W, C, C, C, V,), (G,))
branch_kernel.kinds = ((C, C, C, C, G, W, C,), (C, W,))
gate_kernel.kinds = ((W, C, C, C, C, W,), (C, G, C,))
adjoint_kernel.kinds = ((S, W, C, C, C, C, C, C, G, G, C,), (C, G, G, G, C,))
outs_kernel.kinds = ((W, C, C, C, C, C, C, C, C, G, C, V,), (C, C, G,))
sums_kernel.kinds = ((G, W, C, G, G, G, G, O,), (G,))
finish_kernel.kinds = ((S, G, W, C, C, C, C, C, C, C, C,), (C,))


def shifted(value, step):
    pairs = [(i, i + step) for i in range(64) if 0 <= i + step < 64]
    return lax.ppermute(value, CTX, pairs)


def local(features, conv_weight, log_rate, residues, skip_weight, norm_gain, cotangent):
    feat = features[0].transpose(1, 0, 2)
    taps = conv_weight.transpose(1, 0, 2)
    cot = cotangent[0]
    channels = feat.shape[2]
    groups = log_rate.shape[1]
    count = lax.axis_size(CTX)
    skip = skip_weight[None]
    gain = norm_gain[None]
    where = lax.axis_index(CTX).astype(jnp.int32)[None]

    def call(setup, outs, args, extra=(), flops=0, moved=0, special=0):
        kinds_in, kinds_out = setup.kinds
        fetched = [a for a, k in zip(args, kinds_in) if k not in HELD]
        space = {"smem": pltpu.SMEM, "vmem": pltpu.VMEM}
        return pl.pallas_call(
            functools.partial(streamed, setup, kinds_in, kinds_out),
            in_specs=[pl.BlockSpec(memory_space=space.get(k, pl.ANY)) for k in kinds_in],
            out_specs=[pl.BlockSpec(memory_space=pl.ANY) for _ in outs],
            out_shape=outs,
            scratch_shapes=[pltpu.SemaphoreType.DMA((len(fetched) + len(outs), PARTS))]
            + [pltpu.VMEM(a.shape, a.dtype) for a in [*fetched, *outs]]
            + [pltpu.VMEM(d, F32) for d in extra],
            compiler_params=params(VMEM_MIB),
            cost_estimate=pl.CostEstimate(flops=flops, bytes_accessed=moved, transcendentals=special),
            name=setup.__name__,
        )(*args)

    wide = shape(L, channels)
    per_pole = shape(groups, POLES, GS)
    edges = shape(2, PAD, channels)
    ext3 = (3, PAD + L, GS)

    halo = shifted(feat[:, L - PAD :], 1)
    rate = jnp.exp(log_rate)
    by_pole = jnp.broadcast_to(rate.T[:, :, None], (groups, POLES, GS))
    by_lane = jnp.tile(rate.T, (1, GS // POLES))[:, None, :]

    key, value, ends, edge = call(
        ends_kernel, [wide, wide, per_pole, edges], (by_pole, feat, halo, taps), [ext3]
    )
    near = shifted(edge, -1)

    def owned(rows):
        return lax.all_to_all(rows.reshape(count, 2, GS), CTX, 0, 0).reshape(L, GS)

    def carried(rows, after, back):
        summed = pl.pallas_call(
            functools.partial(scan_kernel, back),
            in_specs=[smem(), smem(), vmem()] + [pl.BlockSpec(memory_space=pl.ANY)] * len(after),
            out_specs=vmem(),
            out_shape=shape(L, GS),
            compiler_params=params(16),
            name="carry_back" if back else "carry_on",
        )(rate, where, rows, *after)
        given = lax.all_to_all(summed.reshape(count, 2, GS), CTX, 0, 0)
        return given.reshape(groups, POLES, GS)

    rows_in = owned(ends)
    coefs = call(
        coefs_kernel,
        [shape(groups, 2 * TAPS * POLES, GS)],
        (by_pole, key, value, feat, halo),
        [ext3],
        flops=4_000_000_000,
        moved=4_000_000,
    )[0]
    state_in = carried(rows_in, (coefs, near), False)

    query, base, states = call(
        states_kernel,
        [wide, wide, shape(POLES, L, channels)],
        (rate, feat, halo, taps, key, value, residues, skip),
        [ext3],
        flops=4_000_000_000,
        moved=14_000_000,
        special=4_000_000,
    )
    branch, stats = call(
        branch_kernel,
        [wide, shape(8, L)],
        (query, base, cot, gain, state_in, by_lane, residues),
        [(2, L, GS)],
    )
    stats = lax.psum(stats, "c")

    dbranch, back_in, edge = call(
        gate_kernel, [wide, per_pole, edges], (stats, query, branch, cot, gain, by_pole)
    )
    rows_back = owned(back_in)
    dlocal, res_part, loc_part, mix_part, edge = call(
        adjoint_kernel,
        [wide, per_pole, per_pole, per_pole, shape(3, PAD, channels)],
        (rate, by_pole, dbranch, key, value, states, residues, skip, state_in, back_in, edge),
        flops=6_000_000_000,
        moved=16_000_000,
        special=4_000_000,
    )
    later = carried(rows_back, (dlocal,), True)
    rim = shifted(edge, -1)

    block_out, dquery, pack = call(
        outs_kernel,
        [shape(L, channels, dtype=BF16), wide, shape(groups, ROWS, GS)],
        (stats, query, branch, cot, gain, key, value, dbranch, dlocal, res_part, feat, halo),
        [ext3],
        flops=1_000_000_000,
        moved=10_000_000,
    )
    pack = call(
        sums_kernel,
        [shape(groups, ROWS, GS)],
        (later, by_pole, residues, loc_part, mix_part, coefs, pack, rim),
    )[0]
    feature_grad = call(
        finish_kernel,
        [shape(3, L, channels, dtype=BF16)],
        (rate, later, by_lane, dlocal, dquery, key, value, residues, rim, near, taps),
        [ext3],
        flops=1_000_000_000,
        moved=10_000_000,
    )[0]

    share = groups * ROWS // count
    parts = lax.all_to_all(pack.reshape(count, share, GS), CTX, 0, 0)
    mine = lax.psum(jnp.sum(parts, axis=0), "y")
    totals = lax.all_to_all(jnp.broadcast_to(mine[None], (count, share, GS)), CTX, 0, 0)
    totals = totals.reshape(groups, ROWS, GS)
    conv, rate_grad, res, skip_grad, gain_grad = pl.pallas_call(
        unpack_kernel,
        out_shape=[shape(3, TAPS, channels), shape(groups, GS), shape(POLES, channels)] + [shape(1, channels)] * 2,
        compiler_params=params(16),
        name="unpack",
    )(totals)
    return (
        block_out[None],
        feature_grad.transpose(1, 0, 2)[None],
        conv.transpose(1, 0, 2),
        rate_grad[:, :POLES].T,
        res,
        skip_grad[0],
        gain_grad[0],
    )


def solution(mesh):
    split_mesh = Mesh(mesh.devices.reshape(4, 4, 16, 2), ("y", "x", "z", "c"))
    in_specs = (
        P("y", CTX, None, "c"),
        P(None, None, "c"),
        P(None, "c"),
        P(None, "c"),
        P("c"),
        P("c"),
        P("y", CTX, "c"),
    )
    out_specs = (
        P("y", CTX, "c"),
        P("y", CTX, None, "c"),
        P(None, None, "c"),
        P(None, "c"),
        P(None, "c"),
        P("c"),
        P("c"),
    )
    return jax.shard_map(local, mesh=split_mesh, in_specs=in_specs, out_specs=out_specs, check_vma=False)
```

```python
import functools
import jax
import jax.numpy as jnp
from jax import lax
from jax.experimental import pallas as pl
from jax.experimental.pallas import tpu as pltpu
from jax.sharding import Mesh
from jax.sharding import PartitionSpec as P

D = 4096
EPSILON = 1e-06
HIGHEST = lax.Precision.HIGHEST
F32 = jnp.float32
BF16 = jnp.bfloat16
L = 128
GS = 128
POLES = 8
TAPS = 7
PAD = 8
GROUPS_HERE = 16
PARTS = 4
HELD = ("smem", "vmem", "order")
C, G, W, S, V, O = "cols", "groups", "whole", "smem", "vmem", "order"
ROWS = 32
VMEM_MIB = 53
ENDS_MIB = 53.6
CTX = ("x", "z")
YX = ("y", "x")


def window(ref, kind, part):
    if kind == "cols":
        span = ref.shape[-1] // PARTS
        at = pl.ds(pl.multiple_of(part * span, span), span)
        return ref.at[(slice(None),) * (len(ref.shape) - 1) + (at,)]
    if kind == "groups":
        span = ref.shape[0] // PARTS
        return ref.at[pl.ds(part * span, span)]
    return ref


def streamed(setup, kinds_in, kinds_out, *refs):
    ins, outs = refs[: len(kinds_in)], refs[len(kinds_in) : len(kinds_in) + len(kinds_out)]
    rest = list(refs[len(kinds_in) + len(kinds_out) :])
    sems, scratch = rest[0], rest[1:]
    moved = [k for k in kinds_in if k not in HELD]
    in_bufs = scratch[: len(moved)]
    out_bufs = scratch[len(moved) : len(moved) + len(kinds_out)]
    extra = scratch[len(moved) + len(kinds_out) :]
    sources = [r for r, k in zip(ins, kinds_in) if k not in HELD]

    def fetch(n, part):
        src, dst = window(sources[n], moved[n], part), window(in_bufs[n], moved[n], part)
        return pltpu.make_async_copy(src, dst, sems.at[n, part])

    def store(n, part):
        src, dst = window(out_bufs[n], kinds_out[n], part), window(outs[n], kinds_out[n], part)
        return pltpu.make_async_copy(src, dst, sems.at[len(moved) + n, part])

    for n, kind in enumerate(moved):
        if kind == "whole":
            fetch(n, 0).start()

    def begin(part, carry):
        for n, kind in enumerate(moved):
            if kind != "whole":
                fetch(n, part).start()
        return carry

    lax.fori_loop(0, PARTS, begin, 0)
    for n, kind in enumerate(moved):
        if kind == "whole":
            fetch(n, 0).wait()
    buffers = iter(in_bufs)
    views = [r if k in HELD else next(buffers) for r, k in zip(ins, kinds_in)]
    body, last = setup(*[v for v, k in zip(views, kinds_in) if k != "order"], *out_bufs, *extra)
    per_part = GROUPS_HERE // PARTS

    def step(part, carry):
        for n, kind in enumerate(moved):
            if kind != "whole":
                fetch(n, part).wait()
        for i in range(per_part):
            gi = part * per_part + i
            body(gi, pl.ds(pl.multiple_of(gi * GS, GS), GS))
        for n, kind in enumerate(kinds_out):
            if kind != "whole":
                store(n, part).start()
        return carry

    lax.fori_loop(0, PARTS, step, 0)
    if last is not None:
        last()
    for n, kind in enumerate(kinds_out):
        if kind == "whole":
            store(n, 0).start()

    def end(part, carry):
        for n, kind in enumerate(kinds_out):
            if kind != "whole":
                store(n, part).wait()
        return carry

    lax.fori_loop(0, PARTS, end, 0)
    for n, kind in enumerate(kinds_out):
        if kind == "whole":
            store(n, 0).wait()


def params(mib):
    return pltpu.CompilerParams(vmem_limit_bytes=int(mib * 1024 * 1024))


def iota(shape, dim):
    return lax.broadcasted_iota(jnp.int32, shape, dim)


def ones_tri(lower):
    row = iota((L, 2 * L), 0)
    col = iota((L, 2 * L), 1) % L
    keep = col <= row if lower else col >= row
    return jnp.where(keep, 1.0, 0.0).astype(BF16)


def powers(rate, sign):
    column = iota((PAD, GS), 0).astype(F32)
    table = jnp.exp((sign * rate) * column)
    rows = PAD
    while rows < L:
        factor = jnp.exp(jnp.full((PAD, GS), sign * rows, F32) * rate)
        more = jnp.concatenate([factor] * (rows // PAD), axis=0)
        table = jnp.concatenate([table, table * more], axis=0)
        rows *= 2
    return table


def split(x):
    high = x.astype(BF16)
    low = (x - high.astype(F32)).astype(BF16)
    return jnp.concatenate([high, low], axis=0)


def tri_dot(tri, xs):
    return jnp.dot(tri, jnp.concatenate([split(x) for x in xs], axis=1), preferred_element_type=F32)


def rowsum(x):
    return jnp.sum(x, axis=0, keepdims=True)


def fill_ext(ext, feat, halo, cs):
    for j in range(3):
        ext[j, 0:PAD, :] = halo[j, :, cs].astype(F32)
        ext[j, PAD : PAD + L, :] = feat[j, :, cs].astype(F32)


def filtered(j, taps, feat, halo, cs, ext):
    ext[j, 0:PAD, :] = halo[j, :, cs].astype(F32)
    ext[j, PAD : PAD + L, :] = feat[j, :, cs].astype(F32)
    acc = taps[j, 0:1, cs] * ext[j, PAD : PAD + L, :]
    for k in range(1, TAPS):
        acc = acc + taps[j, k : k + 1, cs] * ext[j, pl.ds(PAD - k, L), :]
    return acc


def two_parts(table):
    high = table.astype(BF16).astype(F32)
    both = jnp.concatenate([high, table - high], axis=0)
    return jnp.concatenate([both, both], axis=1).astype(BF16)


def weighted_rows(table, x):
    both = jnp.dot(two_parts(table), split(x), preferred_element_type=F32)
    return both[0:POLES, :] + both[POLES : 2 * POLES, :]


def lane_place():
    return iota((POLES, L), 1).astype(F32)


def spread_poles(lane_rate, sign, rows):
    lane = iota((L, 4 * POLES), 1)
    place = iota((L, 4 * POLES), 0).astype(F32)
    steps = place + 1.0 if sign > 0 else L - 1.0 - place
    table = jnp.exp(-steps * lane_rate[:, 0 : 4 * POLES])
    high = table.astype(BF16).astype(F32)
    left = jnp.where((lane // POLES) % 2 == 0, high, table - high).astype(BF16)
    top = rows.astype(BF16).astype(F32)
    low = rows - top
    right = jnp.concatenate([top, top, low, low], axis=0).astype(BF16)
    return jnp.dot(left, right, preferred_element_type=F32)


def ends_kernel(by_pole, feat, halo, taps, k_o, v_o, e_o, edge_o, ext):
    def body(gi, cs):
        key = filtered(1, taps, feat, halo, cs, ext)
        value = filtered(2, taps, feat, halo, cs, ext)
        k_o[:, cs] = key
        v_o[:, cs] = value
        edge_o[0, :, cs] = key[0:PAD, :]
        edge_o[1, :, cs] = value[0:PAD, :]
        e_o[gi] = weighted_rows(jnp.exp(-by_pole[gi] * (L - 1.0 - lane_place())), key * value)

    return body, None


def states_kernel(rate, feat, halo, taps, k, v, weight, skip, q_o, bl_o, s_o, ext):
    tri = ones_tri(True)
    def body(gi, cs):
        q_o[:, cs] = filtered(0, taps, feat, halo, cs, ext)
        prod = k[:, cs] * v[:, cs]
        modal = skip[0:1, cs] * prod
        for p in range(0, POLES, 2):
            rates = [rate[p + i, gi] for i in range(2)]
            both = tri_dot(tri, [powers(r, 1.0) * prod for r in rates])
            for i, r in enumerate(rates):
                state = powers(r, -1.0) * both[:, i * GS : (i + 1) * GS]
                s_o[p + i, :, cs] = state
                modal = modal + weight[p + i : p + i + 1, cs] * state
        bl_o[:, cs] = modal

    return body, None


def coefs_kernel(by_pole, k, v, feat, halo, c_o, ext):
    def body(gi, cs):
        fill_ext(ext, feat, halo, cs)
        table = two_parts(jnp.exp(-by_pole[gi] * (L - 1.0 - lane_place())))
        for j, other in ((1, v[:, cs]), (2, k[:, cs])):
            xs = [split(other * ext[j, pl.ds(PAD - t, L), :]) for t in range(TAPS)]
            both = jnp.dot(table, jnp.concatenate(xs, axis=1), preferred_element_type=F32)
            both = both[0:POLES, :] + both[POLES : 2 * POLES, :]
            for t in range(TAPS):
                at = POLES * (TAPS * (j - 1) + t)
                c_o[gi, at : at + POLES, :] = both[:, t * GS : (t + 1) * GS]

    return body, None


def scan_kernel(back, rate, where, rows, *refs):
    me = where[0]
    group = me // 4
    pole = 2 * (me % 4)
    low, high = rate[pole, group], rate[pole + 1, group]
    row, col = iota((L, L), 0), iota((L, L), 1)
    lag = col // 2 - row // 2 - 1 if back else row // 2 - col // 2 - 1
    keep = (lag >= 0) & (row % 2 == col % 2)
    own = jnp.where(row % 2 == 0, low, high)
    decay = jnp.where(keep, jnp.exp(-(own * L) * jnp.maximum(lag, 0).astype(F32)), 0.0)
    refs[-1][...] = jnp.dot(decay, rows[...], precision=HIGHEST, preferred_element_type=F32)


def branch_kernel(q, bl, cot, gain, state_in, by_lane, weight, br_o, stats_o, acc):
    acc[...] = jnp.zeros_like(acc)

    def body(gi, cs):
        branch = bl[:, cs] + spread_poles(by_lane[gi], 1, weight[:, cs] * state_in[gi])
        br_o[:, cs] = branch
        gated = q[:, cs] * branch
        acc[0] += gated * gated
        acc[1] += (gain[0:1, cs] * cot[:, cs].astype(F32)) * gated

    def last():
        row = iota((8, L), 0)
        squares = rowsum(acc[0].T)
        slopes = rowsum(acc[1].T)
        stats_o[...] = jnp.where(row == 0, squares, jnp.where(row == 1, slopes, 0.0))

    return body, last


def down(row):
    return jnp.broadcast_to(row, (L, L)).T


def gate_kernel(stats, q, br, cot, gain, by_pole, g_o, back_o, edge_o):
    inv_row = lax.rsqrt(stats[0:1, :] / D + EPSILON)
    inv = down(inv_row)
    pull = down(stats[1:2, :] * inv_row * inv_row * inv_row / D)
    def body(gi, cs):
        query, branch = q[:, cs], br[:, cs]
        dgated = (gain[0:1, cs] * cot[:, cs].astype(F32)) * inv - (query * branch) * pull
        dbranch = dgated * query
        g_o[:, cs] = dbranch
        back = weighted_rows(jnp.exp(-by_pole[gi] * (lane_place() + 1.0)), dbranch)
        back_o[gi] = back
        edge_o[0, :, cs] = dgated[0:PAD, :] * branch[0:PAD, :]
        edge_o[1, :, cs] = back

    return body, None


def adjoint_kernel(
    rate, by_pole, g, k, v, states, weight, skip, state_in, back, edge,
    dpl_o, res_o, loc_o, mix_o, edge_o,
):
    tri = ones_tri(False)
    place = iota((L, GS), 0).astype(F32)
    centre = place - (L - 1) / 2
    lane = lane_place()
    def body(gi, cs):
        dbranch = g[:, cs]
        prod = k[:, cs] * v[:, cs]
        total = skip[0:1, cs] * dbranch
        far_grad = centre * dbranch
        far_prod = centre * prod
        own_in = state_in[gi]
        own_rate = by_pole[gi]
        once = jnp.exp(-own_rate)
        residue = own_in * back[gi]
        heavy = weighted_rows((lane + 1.0) * jnp.exp(-own_rate * lane), dbranch)
        deep = weighted_rows((L - 1.0 - lane) * jnp.exp(-own_rate * (L - 2.0 - lane)), prod)
        mix_o[gi] = once * (deep + L * jnp.exp(-(L - 1) * own_rate) * own_in)
        loc = once * own_in * heavy
        for p in range(0, POLES, 2):
            rates = [rate[p + i, gi] for i in range(2)]
            both = tri_dot(tri, [powers(r, -1.0) * dbranch for r in rates])
            for i, r in enumerate(rates):
                at = slice(p + i, p + i + 1)
                adjoint = powers(r, 1.0) * both[:, i * GS : (i + 1) * GS]
                total = total + weight[at, cs] * adjoint
                res_o[gi, at, :] = residue[at, :] + rowsum(prod * adjoint)
                loc_o[gi, at, :] = loc[at, :] + rowsum(far_grad * states[p + i, :, cs] - far_prod * adjoint)
        dpl_o[:, cs] = total
        edge_o[0, :, cs] = edge[0, :, cs]
        edge_o[1, :, cs] = total[0:PAD, :]
        edge_o[2, :, cs] = edge[1, :, cs]

    return body, None


def outs_kernel(
    stats, q, br, cot, gain, k, v, g, dpl, res, feat, halo, out_o, dq_o, pack_o, ext,
):
    inv_row = lax.rsqrt(stats[0:1, :] / D + EPSILON)
    inv = down(inv_row)
    pull = down(stats[1:2, :] * inv_row * inv_row * inv_row / D)
    def body(gi, cs):
        fill_ext(ext, feat, halo, cs)
        query, branch, key, value = q[:, cs], br[:, cs], k[:, cs], v[:, cs]
        grad = cot[:, cs].astype(F32)
        gated = query * branch
        normed = gated * inv
        out_o[:, cs] = (gain[0:1, cs] * normed).astype(BF16)
        dquery = ((gain[0:1, cs] * grad) * inv - gated * pull) * branch
        dq_o[:, cs] = dquery
        local_prod = dpl[:, cs]
        for j, own in enumerate((dquery, local_prod * value, local_prod * key)):
            for t in range(TAPS):
                at = TAPS * j + t
                pack_o[gi, at : at + 1, :] = rowsum(own * ext[j, pl.ds(PAD - t, L), :])
        pack_o[gi, 21:29, :] = res[gi]
        pack_o[gi, 29:30, :] = rowsum(g[:, cs] * (key * value))
        pack_o[gi, 30:31, :] = rowsum(grad * normed)
        pack_o[gi, 31:32, :] = jnp.zeros((1, GS), F32)

    return body, None


def sums_kernel(later, by_pole, weight, loc, mix, coefs, pack, pack_o):
    lane, sub = iota((POLES, GS), 1), iota((POLES, GS), 0)
    def body(gi, cs):
        coming = later[gi]
        scaled = weight[:, cs] * coming
        pack_o[gi] = pack[gi]
        for i in range(2 * TAPS):
            at = TAPS + i
            more = rowsum(scaled * coefs[gi, POLES * i : POLES * (i + 1), :])
            pack_o[gi, at : at + 1, :] = pack[gi, at : at + 1, :] + more
        inner = jnp.sum(weight[:, cs] * (loc[gi] + coming * mix[gi]), axis=1, keepdims=True)
        pack_o[gi, 31:32, :] = rowsum(jnp.where(lane == sub, -by_pole[gi] * inner, 0.0))

    return body, None


def finish_kernel(rate, later, by_lane, dpl, dq, k, v, weight, rim, near, taps, grad_o, dext):
    ahead = (iota((PAD, GS), 0) + 1).astype(F32)
    def body(gi, cs):
        coming = later[gi]
        dprod = dpl[:, cs] + spread_poles(by_lane[gi], -1, weight[:, cs] * coming)
        dext[0, 0:L, :] = dq[:, cs]
        dext[1, 0:L, :] = dprod * v[:, cs]
        dext[2, 0:L, :] = dprod * k[:, cs]
        beyond = weight[:, cs] * (coming - rim[2, :, cs])
        next_prod = rim[1, :, cs]
        for p in range(POLES):
            next_prod = next_prod + jnp.exp(ahead * rate[p, gi]) * beyond[p : p + 1, :]
        dext[0, L : L + PAD, :] = rim[0, :, cs]
        dext[1, L : L + PAD, :] = next_prod * near[1, :, cs]
        dext[2, L : L + PAD, :] = next_prod * near[0, :, cs]
        for j in range(3):
            acc = taps[j, 0:1, cs] * dext[j, 0:L, :]
            for t in range(1, TAPS):
                acc = acc + taps[j, t : t + 1, cs] * dext[j, pl.ds(t, L), :]
            grad_o[j, :, cs] = acc.astype(BF16)

    return body, None


def relay_kernel(parts, _, out):
    out[...] = jnp.broadcast_to(jnp.sum(parts[...], axis=0, keepdims=True), out.shape)


def unpack_kernel(pack, conv_o, rate_o, res_o, skip_o, gain_o):
    groups = pack.shape[0]
    for gi in range(groups):
        cs = slice(gi * GS, (gi + 1) * GS)
        for j in range(3):
            conv_o[j, :, cs] = pack[gi, TAPS * j : TAPS * j + TAPS, :]
        res_o[:, cs] = pack[gi, 21:29, :]
        skip_o[0:1, cs] = pack[gi, 29:30, :]
        gain_o[0:1, cs] = pack[gi, 30:31, :]
        rate_o[gi : gi + 1, :] = pack[gi, 31:32, :]


def smem():
    return pl.BlockSpec(memory_space=pltpu.SMEM)


def vmem():
    return pl.BlockSpec(memory_space=pltpu.VMEM)


def shape(*dims, dtype=F32):
    return jax.ShapeDtypeStruct(dims, dtype)


ends_kernel.kinds = ((W, C, V, C,), (C, C, G, C,))
states_kernel.kinds = ((S, C, V, C, C, C, C, C,), (C, C, C,))
coefs_kernel.kinds = ((W, C, C, C, V,), (G,))
branch_kernel.kinds = ((C, C, C, C, G, W, C,), (C, W,))
gate_kernel.kinds = ((W, C, C, C, C, W,), (C, G, C,))
adjoint_kernel.kinds = ((S, W, C, C, C, C, C, C, G, G, C,), (C, G, G, G, C,))
outs_kernel.kinds = ((W, C, C, C, C, C, C, C, C, G, C, V,), (C, C, G,))
sums_kernel.kinds = ((G, W, C, G, G, G, G, O,), (G,))
finish_kernel.kinds = ((S, G, W, C, C, C, C, C, C, C, C,), (C,))


def shifted(value, step):
    pairs = [(i, i + step) for i in range(64) if 0 <= i + step < 64]
    return lax.ppermute(value, CTX, pairs)


def local(features, conv_weight, log_rate, residues, skip_weight, norm_gain, cotangent):
    feat = features[0].transpose(1, 0, 2)
    taps = conv_weight.transpose(1, 0, 2)
    cot = cotangent[0]
    channels = feat.shape[2]
    groups = log_rate.shape[1]
    count = lax.axis_size(CTX)
    skip = skip_weight[None]
    gain = norm_gain[None]
    where = lax.axis_index(CTX).astype(jnp.int32)[None]

    def call(setup, outs, args, extra=(), flops=0, moved=0, special=0):
        kinds_in, kinds_out = setup.kinds
        fetched = [a for a, k in zip(args, kinds_in) if k not in HELD]
        space = {"smem": pltpu.SMEM, "vmem": pltpu.VMEM}
        return pl.pallas_call(
            functools.partial(streamed, setup, kinds_in, kinds_out),
            in_specs=[pl.BlockSpec(memory_space=space.get(k, pl.ANY)) for k in kinds_in],
            out_specs=[pl.BlockSpec(memory_space=pl.ANY) for _ in outs],
            out_shape=outs,
            scratch_shapes=[pltpu.SemaphoreType.DMA((len(fetched) + len(outs), PARTS))]
            + [pltpu.VMEM(a.shape, a.dtype) for a in [*fetched, *outs]]
            + [pltpu.VMEM(d, F32) for d in extra],
            compiler_params=params(ENDS_MIB if setup is ends_kernel else VMEM_MIB),
            cost_estimate=pl.CostEstimate(flops=flops, bytes_accessed=moved, transcendentals=special),
            name=setup.__name__,
        )(*args)

    wide = shape(L, channels)
    per_pole = shape(groups, POLES, GS)
    edges = shape(2, PAD, channels)
    ext3 = (3, PAD + L, GS)

    halo = shifted(feat[:, L - PAD :], 1)
    rate = jnp.exp(log_rate)
    by_pole = jnp.broadcast_to(rate.T[:, :, None], (groups, POLES, GS))
    by_lane = jnp.tile(rate.T, (1, GS // POLES))[:, None, :]

    key, value, ends, edge = call(
        ends_kernel, [wide, wide, per_pole, edges], (by_pole, feat, halo, taps), [ext3]
    )
    near = shifted(edge, -1)

    def owned(rows):
        return lax.all_to_all(rows.reshape(count, 2, GS), CTX, 0, 0).reshape(L, GS)

    def carried(rows, after, back):
        summed = pl.pallas_call(
            functools.partial(scan_kernel, back),
            in_specs=[smem(), smem(), vmem()] + [pl.BlockSpec(memory_space=pl.ANY)] * len(after),
            out_specs=vmem(),
            out_shape=shape(L, GS),
            compiler_params=params(VMEM_MIB),
            name="carry_back" if back else "carry_on",
        )(rate, where, rows, *after)
        given = lax.all_to_all(summed.reshape(count, 2, GS), CTX, 0, 0)
        return given.reshape(groups, POLES, GS)

    rows_in = owned(ends)
    coefs = call(
        coefs_kernel,
        [shape(groups, 2 * TAPS * POLES, GS)],
        (by_pole, key, value, feat, halo),
        [ext3],
        flops=4_000_000_000,
        moved=4_000_000,
    )[0]
    state_in = carried(rows_in, (coefs, near), False)

    query, base, states = call(
        states_kernel,
        [wide, wide, shape(POLES, L, channels)],
        (rate, feat, halo, taps, key, value, residues, skip),
        [ext3],
        flops=4_000_000_000,
        moved=14_000_000,
        special=4_000_000,
    )
    branch, stats = call(
        branch_kernel,
        [wide, shape(8, L)],
        (query, base, cot, gain, state_in, by_lane, residues),
        [(2, L, GS)],
    )
    stats = lax.psum(stats, "c")

    dbranch, back_in, edge = call(
        gate_kernel, [wide, per_pole, edges], (stats, query, branch, cot, gain, by_pole)
    )
    rows_back = owned(back_in)
    dlocal, res_part, loc_part, mix_part, edge = call(
        adjoint_kernel,
        [wide, per_pole, per_pole, per_pole, shape(3, PAD, channels)],
        (rate, by_pole, dbranch, key, value, states, residues, skip, state_in, back_in, edge),
        flops=6_000_000_000,
        moved=16_000_000,
        special=4_000_000,
    )
    later = carried(rows_back, (loc_part,), True)
    rim = shifted(edge, -1)

    block_out, dquery, pack = call(
        outs_kernel,
        [shape(L, channels, dtype=BF16), wide, shape(groups, ROWS, GS)],
        (stats, query, branch, cot, gain, key, value, dbranch, dlocal, res_part, feat, halo),
        [ext3],
        flops=1_000_000_000,
        moved=10_000_000,
    )
    pack = call(
        sums_kernel,
        [shape(groups, ROWS, GS)],
        (later, by_pole, residues, loc_part, mix_part, coefs, pack, rim),
    )[0]
    feature_grad = call(
        finish_kernel,
        [shape(3, L, channels, dtype=BF16)],
        (rate, later, by_lane, dlocal, dquery, key, value, residues, rim, near, taps),
        [ext3],
        flops=1_000_000_000,
        moved=10_000_000,
    )[0]

    owned_rows = jnp.sum(lax.all_to_all(pack, YX, 0, 0), axis=0)
    depth = lax.axis_size("z")
    slices = owned_rows.reshape(depth, ROWS // depth, GS)
    copies = pl.pallas_call(
        relay_kernel,
        in_specs=[vmem(), pl.BlockSpec(memory_space=pl.ANY)],
        out_specs=vmem(),
        out_shape=shape(*slices.shape),
        compiler_params=params(VMEM_MIB),
        name="relay",
    )(lax.all_to_all(slices, "z", 0, 0), feature_grad)
    whole = lax.all_to_all(copies, "z", 0, 0).reshape(ROWS, GS)
    totals = lax.all_to_all(jnp.broadcast_to(whole[None], pack.shape), YX, 0, 0)
    conv, rate_grad, res, skip_grad, gain_grad = pl.pallas_call(
        unpack_kernel,
        out_shape=[shape(3, TAPS, channels), shape(groups, GS), shape(POLES, channels)] + [shape(1, channels)] * 2,
        compiler_params=params(16),
        name="unpack",
    )(totals)
    return (
        block_out[None],
        feature_grad.transpose(1, 0, 2)[None],
        conv.transpose(1, 0, 2),
        rate_grad[:, :POLES].T,
        res,
        skip_grad[0],
        gain_grad[0],
    )


def solution(mesh):
    split_mesh = Mesh(mesh.devices.reshape(4, 4, 16, 2), ("y", "x", "z", "c"))
    in_specs = (
        P("y", CTX, None, "c"),
        P(None, None, "c"),
        P(None, "c"),
        P(None, "c"),
        P("c"),
        P("c"),
        P("y", CTX, "c"),
    )
    out_specs = (
        P("y", CTX, "c"),
        P("y", CTX, None, "c"),
        P(None, None, "c"),
        P(None, "c"),
        P(None, "c"),
        P("c"),
        P("c"),
    )
    return jax.shard_map(local, mesh=split_mesh, in_specs=in_specs, out_specs=out_specs, check_vma=False)
```

```python
import functools
import jax
import jax.numpy as jnp
from jax import lax
from jax.experimental import pallas as pl
from jax.experimental.pallas import tpu as pltpu
from jax.sharding import Mesh
from jax.sharding import PartitionSpec as P

D = 4096
EPSILON = 1e-06
HIGHEST = lax.Precision.HIGHEST
F32 = jnp.float32
BF16 = jnp.bfloat16
L = 128
GS = 128
POLES = 8
TAPS = 7
PAD = 8
GROUPS_HERE = 16
PARTS = 4
HELD = ("smem", "vmem", "order")
C, G, W, S, V, O = "cols", "groups", "whole", "smem", "vmem", "order"
ROWS = 32
VMEM_MIB = 53
ENDS_MIB = 53.6
CTX = ("x", "z")
YX = ("y", "x")


def window(ref, kind, part):
    if kind == "cols":
        span = ref.shape[-1] // PARTS
        at = pl.ds(pl.multiple_of(part * span, span), span)
        return ref.at[(slice(None),) * (len(ref.shape) - 1) + (at,)]
    if kind == "groups":
        span = ref.shape[0] // PARTS
        return ref.at[pl.ds(part * span, span)]
    return ref


def streamed(setup, kinds_in, kinds_out, *refs):
    ins, outs = refs[: len(kinds_in)], refs[len(kinds_in) : len(kinds_in) + len(kinds_out)]
    rest = list(refs[len(kinds_in) + len(kinds_out) :])
    sems, scratch = rest[0], rest[1:]
    moved = [k for k in kinds_in if k not in HELD]
    in_bufs = scratch[: len(moved)]
    out_bufs = scratch[len(moved) : len(moved) + len(kinds_out)]
    extra = scratch[len(moved) + len(kinds_out) :]
    sources = [r for r, k in zip(ins, kinds_in) if k not in HELD]

    def fetch(n, part):
        src, dst = window(sources[n], moved[n], part), window(in_bufs[n], moved[n], part)
        return pltpu.make_async_copy(src, dst, sems.at[n, part])

    def store(n, part):
        src, dst = window(out_bufs[n], kinds_out[n], part), window(outs[n], kinds_out[n], part)
        return pltpu.make_async_copy(src, dst, sems.at[len(moved) + n, part])

    for n, kind in enumerate(moved):
        if kind == "whole":
            fetch(n, 0).start()

    def begin(part, carry):
        for n, kind in enumerate(moved):
            if kind != "whole":
                fetch(n, part).start()
        return carry

    lax.fori_loop(0, PARTS, begin, 0)
    for n, kind in enumerate(moved):
        if kind == "whole":
            fetch(n, 0).wait()
    buffers = iter(in_bufs)
    views = [r if k in HELD else next(buffers) for r, k in zip(ins, kinds_in)]
    body, last = setup(*[v for v, k in zip(views, kinds_in) if k != "order"], *out_bufs, *extra)
    per_part = GROUPS_HERE // PARTS

    def step(part, carry):
        for n, kind in enumerate(moved):
            if kind != "whole":
                fetch(n, part).wait()
        for i in range(per_part):
            gi = part * per_part + i
            body(gi, pl.ds(pl.multiple_of(gi * GS, GS), GS))
        for n, kind in enumerate(kinds_out):
            if kind != "whole":
                store(n, part).start()
        return carry

    lax.fori_loop(0, PARTS, step, 0)
    if last is not None:
        last()
    for n, kind in enumerate(kinds_out):
        if kind == "whole":
            store(n, 0).start()

    def end(part, carry):
        for n, kind in enumerate(kinds_out):
            if kind != "whole":
                store(n, part).wait()
        return carry

    lax.fori_loop(0, PARTS, end, 0)
    for n, kind in enumerate(kinds_out):
        if kind == "whole":
            store(n, 0).wait()


def params(mib):
    return pltpu.CompilerParams(vmem_limit_bytes=int(mib * 1024 * 1024))


def iota(shape, dim):
    return lax.broadcasted_iota(jnp.int32, shape, dim)


def ones_tri(lower):
    row = iota((L, 2 * L), 0)
    col = iota((L, 2 * L), 1) % L
    keep = col <= row if lower else col >= row
    return jnp.where(keep, 1.0, 0.0).astype(BF16)


def powers(rate, sign):
    column = iota((PAD, GS), 0).astype(F32)
    table = jnp.exp((sign * rate) * column)
    rows = PAD
    while rows < L:
        factor = jnp.exp(jnp.full((PAD, GS), sign * rows, F32) * rate)
        more = jnp.concatenate([factor] * (rows // PAD), axis=0)
        table = jnp.concatenate([table, table * more], axis=0)
        rows *= 2
    return table


def split(x):
    high = x.astype(BF16)
    low = (x - high.astype(F32)).astype(BF16)
    return jnp.concatenate([high, low], axis=0)


def tri_dot(tri, xs):
    return jnp.dot(tri, jnp.concatenate([split(x) for x in xs], axis=1), preferred_element_type=F32)


def rowsum(x):
    return jnp.sum(x, axis=0, keepdims=True)


def fill_ext(ext, feat, halo, cs):
    for j in range(3):
        ext[j, 0:PAD, :] = halo[j, :, cs].astype(F32)
        ext[j, PAD : PAD + L, :] = feat[j, :, cs].astype(F32)


def filtered(j, taps, feat, halo, cs, ext):
    ext[j, 0:PAD, :] = halo[j, :, cs].astype(F32)
    ext[j, PAD : PAD + L, :] = feat[j, :, cs].astype(F32)
    acc = taps[j, 0:1, cs] * ext[j, PAD : PAD + L, :]
    for k in range(1, TAPS):
        acc = acc + taps[j, k : k + 1, cs] * ext[j, pl.ds(PAD - k, L), :]
    return acc


def two_parts(table):
    high = table.astype(BF16).astype(F32)
    both = jnp.concatenate([high, table - high], axis=0)
    return jnp.concatenate([both, both], axis=1).astype(BF16)


def weighted_rows(table, x):
    both = jnp.dot(two_parts(table), split(x), preferred_element_type=F32)
    return both[0:POLES, :] + both[POLES : 2 * POLES, :]


def lane_place():
    return iota((POLES, L), 1).astype(F32)


def spread_poles(lane_rate, sign, rows):
    lane = iota((L, 4 * POLES), 1)
    place = iota((L, 4 * POLES), 0).astype(F32)
    steps = place + 1.0 if sign > 0 else L - 1.0 - place
    table = jnp.exp(-steps * lane_rate[:, 0 : 4 * POLES])
    high = table.astype(BF16).astype(F32)
    left = jnp.where((lane // POLES) % 2 == 0, high, table - high).astype(BF16)
    top = rows.astype(BF16).astype(F32)
    low = rows - top
    right = jnp.concatenate([top, top, low, low], axis=0).astype(BF16)
    return jnp.dot(left, right, preferred_element_type=F32)


def ends_kernel(by_pole, feat, halo, taps, k_o, v_o, e_o, edge_o, ext):
    def body(gi, cs):
        key = filtered(1, taps, feat, halo, cs, ext)
        value = filtered(2, taps, feat, halo, cs, ext)
        k_o[:, cs] = key
        v_o[:, cs] = value
        edge_o[0, :, cs] = key[0:PAD, :]
        edge_o[1, :, cs] = value[0:PAD, :]
        e_o[gi] = weighted_rows(jnp.exp(-by_pole[gi] * (L - 1.0 - lane_place())), key * value)

    return body, None


def states_kernel(rate, feat, halo, taps, k, v, weight, skip, q_o, bl_o, s_o, ext):
    tri = ones_tri(True)
    def body(gi, cs):
        q_o[:, cs] = filtered(0, taps, feat, halo, cs, ext)
        prod = k[:, cs] * v[:, cs]
        modal = skip[0:1, cs] * prod
        for p in range(0, POLES, 2):
            rates = [rate[p + i, gi] for i in range(2)]
            both = tri_dot(tri, [powers(r, 1.0) * prod for r in rates])
            for i, r in enumerate(rates):
                state = powers(r, -1.0) * both[:, i * GS : (i + 1) * GS]
                s_o[p + i, :, cs] = state
                modal = modal + weight[p + i : p + i + 1, cs] * state
        bl_o[:, cs] = modal

    return body, None


def coefs_kernel(by_pole, k, v, feat, halo, c_o, ext):
    def body(gi, cs):
        fill_ext(ext, feat, halo, cs)
        table = two_parts(jnp.exp(-by_pole[gi] * (L - 1.0 - lane_place())))
        for j, other in ((1, v[:, cs]), (2, k[:, cs])):
            xs = [split(other * ext[j, pl.ds(PAD - t, L), :]) for t in range(TAPS)]
            both = jnp.dot(table, jnp.concatenate(xs, axis=1), preferred_element_type=F32)
            both = both[0:POLES, :] + both[POLES : 2 * POLES, :]
            for t in range(TAPS):
                at = POLES * (TAPS * (j - 1) + t)
                c_o[gi, at : at + POLES, :] = both[:, t * GS : (t + 1) * GS]

    return body, None


def scan_kernel(back, rate, where, rows, *refs):
    me = where[0]
    group = me // 4
    pole = 2 * (me % 4)
    low, high = rate[pole, group], rate[pole + 1, group]
    row, col = iota((L, L), 0), iota((L, L), 1)
    lag = col // 2 - row // 2 - 1 if back else row // 2 - col // 2 - 1
    keep = (lag >= 0) & (row % 2 == col % 2)
    own = jnp.where(row % 2 == 0, low, high)
    decay = jnp.where(keep, jnp.exp(-(own * L) * jnp.maximum(lag, 0).astype(F32)), 0.0)
    refs[-1][...] = jnp.dot(decay, rows[...], precision=HIGHEST, preferred_element_type=F32)


def branch_kernel(q, bl, cot, gain, state_in, by_lane, weight, br_o, stats_o, acc):
    acc[...] = jnp.zeros_like(acc)

    def body(gi, cs):
        branch = bl[:, cs] + spread_poles(by_lane[gi], 1, weight[:, cs] * state_in[gi])
        br_o[:, cs] = branch
        gated = q[:, cs] * branch
        acc[0] += gated * gated
        acc[1] += (gain[0:1, cs] * cot[:, cs].astype(F32)) * gated

    def last():
        row = iota((8, L), 0)
        squares = rowsum(acc[0].T)
        slopes = rowsum(acc[1].T)
        stats_o[...] = jnp.where(row == 0, squares, jnp.where(row == 1, slopes, 0.0))

    return body, last


def down(row):
    return jnp.broadcast_to(row, (L, L)).T


def gate_kernel(stats, q, br, cot, gain, by_pole, g_o, back_o, edge_o):
    inv_row = lax.rsqrt(stats[0:1, :] / D + EPSILON)
    inv = down(inv_row)
    pull = down(stats[1:2, :] * inv_row * inv_row * inv_row / D)
    def body(gi, cs):
        query, branch = q[:, cs], br[:, cs]
        dgated = (gain[0:1, cs] * cot[:, cs].astype(F32)) * inv - (query * branch) * pull
        dbranch = dgated * query
        g_o[:, cs] = dbranch
        back = weighted_rows(jnp.exp(-by_pole[gi] * (lane_place() + 1.0)), dbranch)
        back_o[gi] = back
        edge_o[0, :, cs] = dgated[0:PAD, :] * branch[0:PAD, :]
        edge_o[1, :, cs] = back

    return body, None


def adjoint_kernel(
    rate, by_pole, g, k, v, states, weight, skip, state_in, back, edge,
    dpl_o, res_o, loc_o, mix_o, edge_o,
):
    tri = ones_tri(False)
    place = iota((L, GS), 0).astype(F32)
    centre = place - (L - 1) / 2
    lane = lane_place()
    def body(gi, cs):
        dbranch = g[:, cs]
        prod = k[:, cs] * v[:, cs]
        total = skip[0:1, cs] * dbranch
        far_grad = centre * dbranch
        far_prod = centre * prod
        own_in = state_in[gi]
        own_rate = by_pole[gi]
        once = jnp.exp(-own_rate)
        residue = own_in * back[gi]
        heavy = weighted_rows((lane + 1.0) * jnp.exp(-own_rate * lane), dbranch)
        deep = weighted_rows((L - 1.0 - lane) * jnp.exp(-own_rate * (L - 2.0 - lane)), prod)
        mix_o[gi] = once * (deep + L * jnp.exp(-(L - 1) * own_rate) * own_in)
        loc = once * own_in * heavy
        for p in range(0, POLES, 2):
            rates = [rate[p + i, gi] for i in range(2)]
            both = tri_dot(tri, [powers(r, -1.0) * dbranch for r in rates])
            for i, r in enumerate(rates):
                at = slice(p + i, p + i + 1)
                adjoint = powers(r, 1.0) * both[:, i * GS : (i + 1) * GS]
                total = total + weight[at, cs] * adjoint
                res_o[gi, at, :] = residue[at, :] + rowsum(prod * adjoint)
                loc_o[gi, at, :] = loc[at, :] + rowsum(far_grad * states[p + i, :, cs] - far_prod * adjoint)
        dpl_o[:, cs] = total
        edge_o[0, :, cs] = edge[0, :, cs]
        edge_o[1, :, cs] = total[0:PAD, :]
        edge_o[2, :, cs] = edge[1, :, cs]

    return body, None


def outs_kernel(
    stats, q, br, cot, gain, k, v, g, dpl, res, feat, halo, out_o, dq_o, pack_o, ext,
):
    inv_row = lax.rsqrt(stats[0:1, :] / D + EPSILON)
    inv = down(inv_row)
    pull = down(stats[1:2, :] * inv_row * inv_row * inv_row / D)
    def body(gi, cs):
        fill_ext(ext, feat, halo, cs)
        query, branch, key, value = q[:, cs], br[:, cs], k[:, cs], v[:, cs]
        grad = cot[:, cs].astype(F32)
        gated = query * branch
        normed = gated * inv
        out_o[:, cs] = (gain[0:1, cs] * normed).astype(BF16)
        dquery = ((gain[0:1, cs] * grad) * inv - gated * pull) * branch
        dq_o[:, cs] = dquery
        local_prod = dpl[:, cs]
        for j, own in enumerate((dquery, local_prod * value, local_prod * key)):
            for t in range(TAPS):
                at = TAPS * j + t
                pack_o[gi, at : at + 1, :] = rowsum(own * ext[j, pl.ds(PAD - t, L), :])
        pack_o[gi, 21:29, :] = res[gi]
        pack_o[gi, 29:30, :] = rowsum(g[:, cs] * (key * value))
        pack_o[gi, 30:31, :] = rowsum(grad * normed)
        pack_o[gi, 31:32, :] = jnp.zeros((1, GS), F32)

    return body, None


def sums_kernel(later, by_pole, weight, loc, mix, coefs, pack, pack_o):
    lane, sub = iota((POLES, GS), 1), iota((POLES, GS), 0)
    def body(gi, cs):
        coming = later[gi]
        scaled = weight[:, cs] * coming
        pack_o[gi] = pack[gi]
        for i in range(2 * TAPS):
            at = TAPS + i
            more = rowsum(scaled * coefs[gi, POLES * i : POLES * (i + 1), :])
            pack_o[gi, at : at + 1, :] = pack[gi, at : at + 1, :] + more
        inner = jnp.sum(weight[:, cs] * (loc[gi] + coming * mix[gi]), axis=1, keepdims=True)
        pack_o[gi, 31:32, :] = rowsum(jnp.where(lane == sub, -by_pole[gi] * inner, 0.0))

    return body, None


def finish_kernel(rate, later, by_lane, dpl, dq, k, v, weight, rim, near, taps, grad_o, dext):
    ahead = (iota((PAD, GS), 0) + 1).astype(F32)
    def body(gi, cs):
        coming = later[gi]
        dprod = dpl[:, cs] + spread_poles(by_lane[gi], -1, weight[:, cs] * coming)
        dext[0, 0:L, :] = dq[:, cs]
        dext[1, 0:L, :] = dprod * v[:, cs]
        dext[2, 0:L, :] = dprod * k[:, cs]
        beyond = weight[:, cs] * (coming - rim[2, :, cs])
        next_prod = rim[1, :, cs]
        for p in range(POLES):
            next_prod = next_prod + jnp.exp(ahead * rate[p, gi]) * beyond[p : p + 1, :]
        dext[0, L : L + PAD, :] = rim[0, :, cs]
        dext[1, L : L + PAD, :] = next_prod * near[1, :, cs]
        dext[2, L : L + PAD, :] = next_prod * near[0, :, cs]
        for j in range(3):
            acc = taps[j, 0:1, cs] * dext[j, 0:L, :]
            for t in range(1, TAPS):
                acc = acc + taps[j, t : t + 1, cs] * dext[j, pl.ds(t, L), :]
            grad_o[j, :, cs] = acc.astype(BF16)

    return body, None


def relay_kernel(parts, *refs):
    out = refs[-1]
    out[...] = jnp.broadcast_to(jnp.sum(parts[...], axis=0, keepdims=True), out.shape)


def unpack_kernel(pack, conv_o, rate_o, res_o, skip_o, gain_o):
    groups = pack.shape[0]
    for gi in range(groups):
        cs = slice(gi * GS, (gi + 1) * GS)
        for j in range(3):
            conv_o[j, :, cs] = pack[gi, TAPS * j : TAPS * j + TAPS, :]
        res_o[:, cs] = pack[gi, 21:29, :]
        skip_o[0:1, cs] = pack[gi, 29:30, :]
        gain_o[0:1, cs] = pack[gi, 30:31, :]
    rates = jnp.concatenate([pack[gi, 31:32, :] for gi in range(groups)], axis=0)
    rate_o[...] = rates.T[0:POLES, :]


def smem():
    return pl.BlockSpec(memory_space=pltpu.SMEM)


def vmem():
    return pl.BlockSpec(memory_space=pltpu.VMEM)


def shape(*dims, dtype=F32):
    return jax.ShapeDtypeStruct(dims, dtype)


ends_kernel.kinds = ((W, C, V, C,), (C, C, G, C,))
states_kernel.kinds = ((S, C, V, C, C, C, C, C,), (C, C, C,))
coefs_kernel.kinds = ((W, C, C, C, V,), (G,))
branch_kernel.kinds = ((C, C, C, C, G, W, C,), (C, W,))
gate_kernel.kinds = ((W, C, C, C, C, W,), (C, G, C,))
adjoint_kernel.kinds = ((S, W, C, C, C, C, C, C, G, G, C,), (C, G, G, G, C,))
outs_kernel.kinds = ((W, C, C, C, C, C, C, C, C, G, C, V,), (C, C, G,))
sums_kernel.kinds = ((G, W, C, G, G, G, G, O,), (G,))
finish_kernel.kinds = ((S, G, W, C, C, C, C, C, C, C, C,), (C,))


def shifted(value, step):
    pairs = [(i, i + step) for i in range(64) if 0 <= i + step < 64]
    return lax.ppermute(value, CTX, pairs)


def local(features, conv_weight, log_rate, residues, skip_weight, norm_gain, cotangent):
    feat = features[0].transpose(1, 0, 2)
    taps = conv_weight.transpose(1, 0, 2)
    cot = cotangent[0]
    channels = feat.shape[2]
    groups = log_rate.shape[1]
    count = lax.axis_size(CTX)
    skip = skip_weight[None]
    gain = norm_gain[None]
    where = lax.axis_index(CTX).astype(jnp.int32)[None]

    def call(setup, outs, args, extra=(), flops=0, moved=0, special=0):
        kinds_in, kinds_out = setup.kinds
        fetched = [a for a, k in zip(args, kinds_in) if k not in HELD]
        space = {"smem": pltpu.SMEM, "vmem": pltpu.VMEM}
        return pl.pallas_call(
            functools.partial(streamed, setup, kinds_in, kinds_out),
            in_specs=[pl.BlockSpec(memory_space=space.get(k, pl.ANY)) for k in kinds_in],
            out_specs=[pl.BlockSpec(memory_space=pl.ANY) for _ in outs],
            out_shape=outs,
            scratch_shapes=[pltpu.SemaphoreType.DMA((len(fetched) + len(outs), PARTS))]
            + [pltpu.VMEM(a.shape, a.dtype) for a in [*fetched, *outs]]
            + [pltpu.VMEM(d, F32) for d in extra],
            compiler_params=params(ENDS_MIB if setup is ends_kernel else VMEM_MIB),
            cost_estimate=pl.CostEstimate(flops=flops, bytes_accessed=moved, transcendentals=special),
            name=setup.__name__,
        )(*args)

    wide = shape(L, channels)
    per_pole = shape(groups, POLES, GS)
    edges = shape(2, PAD, channels)
    ext3 = (3, PAD + L, GS)

    halo = shifted(feat[:, L - PAD :], 1)
    rate = jnp.exp(log_rate)
    by_pole = jnp.broadcast_to(rate.T[:, :, None], (groups, POLES, GS))
    by_lane = jnp.tile(rate.T, (1, GS // POLES))[:, None, :]

    key, value, ends, edge = call(
        ends_kernel, [wide, wide, per_pole, edges], (by_pole, feat, halo, taps), [ext3]
    )
    near = shifted(edge, -1)

    def owned(rows):
        return lax.all_to_all(rows.reshape(count, 2, GS), CTX, 0, 0).reshape(L, GS)

    def carried(rows, after, back):
        summed = pl.pallas_call(
            functools.partial(scan_kernel, back),
            in_specs=[smem(), smem(), vmem()] + [pl.BlockSpec(memory_space=pl.ANY)] * len(after),
            out_specs=vmem(),
            out_shape=shape(L, GS),
            compiler_params=params(VMEM_MIB),
            name="carry_back" if back else "carry_on",
        )(rate, where, rows, *after)
        given = lax.all_to_all(summed.reshape(count, 2, GS), CTX, 0, 0)
        return given.reshape(groups, POLES, GS)

    rows_in = owned(ends)
    coefs = call(
        coefs_kernel,
        [shape(groups, 2 * TAPS * POLES, GS)],
        (by_pole, key, value, feat, halo),
        [ext3],
        flops=4_000_000_000,
        moved=4_000_000,
    )[0]
    state_in = carried(rows_in, (coefs, near), False)

    query, base, states = call(
        states_kernel,
        [wide, wide, shape(POLES, L, channels)],
        (rate, feat, halo, taps, key, value, residues, skip),
        [ext3],
        flops=4_000_000_000,
        moved=14_000_000,
        special=4_000_000,
    )
    branch, stats = call(
        branch_kernel,
        [wide, shape(8, L)],
        (query, base, cot, gain, state_in, by_lane, residues),
        [(2, L, GS)],
    )
    stats = lax.psum(stats, "c")

    dbranch, back_in, edge = call(
        gate_kernel, [wide, per_pole, edges], (stats, query, branch, cot, gain, by_pole)
    )
    rows_back = owned(back_in)
    dlocal, res_part, loc_part, mix_part, edge = call(
        adjoint_kernel,
        [wide, per_pole, per_pole, per_pole, shape(3, PAD, channels)],
        (rate, by_pole, dbranch, key, value, states, residues, skip, state_in, back_in, edge),
        flops=6_000_000_000,
        moved=16_000_000,
        special=4_000_000,
    )
    later = carried(rows_back, (loc_part,), True)
    rim = shifted(edge, -1)

    block_out, dquery, pack = call(
        outs_kernel,
        [shape(L, channels, dtype=BF16), wide, shape(groups, ROWS, GS)],
        (stats, query, branch, cot, gain, key, value, dbranch, dlocal, res_part, feat, halo),
        [ext3],
        flops=1_000_000_000,
        moved=10_000_000,
    )
    pack = call(
        sums_kernel,
        [shape(groups, ROWS, GS)],
        (later, by_pole, residues, loc_part, mix_part, coefs, pack, rim),
    )[0]
    feature_grad = call(
        finish_kernel,
        [shape(3, L, channels, dtype=BF16)],
        (rate, later, by_lane, dlocal, dquery, key, value, residues, rim, near, taps),
        [ext3],
        flops=1_000_000_000,
        moved=10_000_000,
    )[0]

    def summed_copies(parts, after, name):
        return pl.pallas_call(
            relay_kernel,
            in_specs=[vmem()] + [pl.BlockSpec(memory_space=pl.ANY)] * len(after),
            out_specs=vmem(),
            out_shape=shape(*parts.shape),
            compiler_params=params(VMEM_MIB),
            name=name,
        )(parts, *after)

    owned_rows = summed_copies(lax.all_to_all(pack, YX, 0, 0), (), "add_over_yx")
    everyone = lax.all_to_all(owned_rows, "z", 0, 0)
    totals = lax.all_to_all(summed_copies(everyone, (feature_grad,), "add_over_z"), YX, 0, 0)
    conv, rate_grad, res, skip_grad, gain_grad = pl.pallas_call(
        unpack_kernel,
        out_shape=[shape(3, TAPS, channels), shape(POLES, groups), shape(POLES, channels)] + [shape(1, channels)] * 2,
        compiler_params=params(16),
        name="unpack",
    )(totals)
    return (
        block_out[None],
        feature_grad.transpose(1, 0, 2)[None],
        conv.transpose(1, 0, 2),
        rate_grad,
        res,
        skip_grad[0],
        gain_grad[0],
    )


def solution(mesh):
    split_mesh = Mesh(mesh.devices.reshape(4, 4, 16, 2), ("y", "x", "z", "c"))
    in_specs = (
        P("y", CTX, None, "c"),
        P(None, None, "c"),
        P(None, "c"),
        P(None, "c"),
        P("c"),
        P("c"),
        P("y", CTX, "c"),
    )
    out_specs = (
        P("y", CTX, "c"),
        P("y", CTX, None, "c"),
        P(None, None, "c"),
        P(None, "c"),
        P(None, "c"),
        P("c"),
        P("c"),
    )
    return jax.shard_map(local, mesh=split_mesh, in_specs=in_specs, out_specs=out_specs, check_vma=False)
```

```python
import functools
import jax
import jax.numpy as jnp
from jax import lax
from jax.experimental import pallas as pl
from jax.experimental.pallas import tpu as pltpu
from jax.sharding import Mesh
from jax.sharding import PartitionSpec as P

D = 4096
EPSILON = 1e-06
HIGHEST = lax.Precision.HIGHEST
F32 = jnp.float32
BF16 = jnp.bfloat16
L = 128
GS = 128
POLES = 8
TAPS = 7
PAD = 8
GROUPS_HERE = 16
PARTS = 4
HELD = ("smem", "vmem", "order")
STREAMS = {"first": slice(0, 1), "last": slice(1, 3)}
F0, F12 = "first", "last"
C, G, W, S, V, O = "cols", "groups", "whole", "smem", "vmem", "order"
ROWS = 32
VMEM_MIB = 53
ENDS_MIB = 53.6
OUTS_MIB = 53
CTX = ("x", "z")
YX = ("y", "x")


def window(ref, kind, part):
    if kind == "cols":
        span = ref.shape[-1] // PARTS
        at = pl.ds(pl.multiple_of(part * span, span), span)
        return ref.at[(slice(None),) * (len(ref.shape) - 1) + (at,)]
    if kind in STREAMS:
        span = ref.shape[-1] // PARTS
        return ref.at[STREAMS[kind], :, pl.ds(pl.multiple_of(part * span, span), span)]
    if kind == "groups":
        span = ref.shape[0] // PARTS
        return ref.at[pl.ds(part * span, span)]
    return ref


def streamed(setup, kinds_in, kinds_out, *refs):
    ins, outs = refs[: len(kinds_in)], refs[len(kinds_in) : len(kinds_in) + len(kinds_out)]
    rest = list(refs[len(kinds_in) + len(kinds_out) :])
    sems, scratch = rest[0], rest[1:]
    moved = [k for k in kinds_in if k not in HELD]
    in_bufs = scratch[: len(moved)]
    out_bufs = scratch[len(moved) : len(moved) + len(kinds_out)]
    extra = scratch[len(moved) + len(kinds_out) :]
    sources = [r for r, k in zip(ins, kinds_in) if k not in HELD]

    def fetch(n, part):
        src, dst = window(sources[n], moved[n], part), window(in_bufs[n], moved[n], part)
        return pltpu.make_async_copy(src, dst, sems.at[n, part])

    def store(n, part):
        src, dst = window(out_bufs[n], kinds_out[n], part), window(outs[n], kinds_out[n], part)
        return pltpu.make_async_copy(src, dst, sems.at[len(moved) + n, part])

    for n, kind in enumerate(moved):
        if kind == "whole":
            fetch(n, 0).start()

    def begin(part, carry):
        for n, kind in enumerate(moved):
            if kind != "whole":
                fetch(n, part).start()
        return carry

    lax.fori_loop(0, PARTS, begin, 0)
    for n, kind in enumerate(moved):
        if kind == "whole":
            fetch(n, 0).wait()
    buffers = iter(in_bufs)
    views = [r if k in HELD else next(buffers) for r, k in zip(ins, kinds_in)]
    body, last = setup(*[v for v, k in zip(views, kinds_in) if k != "order"], *out_bufs, *extra)
    per_part = GROUPS_HERE // PARTS

    def step(part, carry):
        for n, kind in enumerate(moved):
            if kind != "whole":
                fetch(n, part).wait()
        for i in range(per_part):
            gi = part * per_part + i
            body(gi, pl.ds(pl.multiple_of(gi * GS, GS), GS))
        for n, kind in enumerate(kinds_out):
            if kind != "whole":
                store(n, part).start()
        return carry

    lax.fori_loop(0, PARTS, step, 0)
    if last is not None:
        last()
    for n, kind in enumerate(kinds_out):
        if kind == "whole":
            store(n, 0).start()

    def end(part, carry):
        for n, kind in enumerate(kinds_out):
            if kind != "whole":
                store(n, part).wait()
        return carry

    lax.fori_loop(0, PARTS, end, 0)
    for n, kind in enumerate(kinds_out):
        if kind == "whole":
            store(n, 0).wait()


def params(mib):
    return pltpu.CompilerParams(vmem_limit_bytes=int(mib * 1024 * 1024))


def iota(shape, dim):
    return lax.broadcasted_iota(jnp.int32, shape, dim)


def ones_tri():
    row = iota((L, 2 * L), 0)
    col = iota((L, 2 * L), 1) % L
    return jnp.where(col <= row, 1.0, 0.0).astype(BF16)


def ones_and_lags():
    row = iota((L, 2 * L), 0)
    col = iota((L, 2 * L), 1) % L
    ones = jnp.where(col >= row, 1.0, 0.0)
    return jnp.concatenate([ones, jnp.maximum(col - row, 0).astype(F32)], axis=0).astype(BF16)


def powers(rates, sign):
    column = iota((PAD, GS), 0).astype(F32)
    spans = [PAD * 2**n for n in range(4)]
    factors = [jnp.exp((sign * span) * rates) for span in spans]
    tables = []
    for p in range(POLES):
        table = jnp.exp((sign * column) * rates[p : p + 1, :])
        for factor in factors:
            table = jnp.concatenate([table, table * factor[p : p + 1, :]], axis=0)
        tables.append(table)
    return tables


def split(x):
    high = x.astype(BF16)
    low = (x - high.astype(F32)).astype(BF16)
    return jnp.concatenate([high, low], axis=0)


def tri_dot(tri, xs):
    return jnp.dot(tri, jnp.concatenate([split(x) for x in xs], axis=1), preferred_element_type=F32)


def rowsum(x):
    return jnp.sum(x, axis=0, keepdims=True)


def extend(j, feat, halo, cs, ext):
    ext[j, 0:PAD, :] = halo[j, :, cs].astype(F32)
    ext[j, PAD : PAD + L, :] = feat[j, :, cs].astype(F32)


def filtered(j, taps, feat, halo, cs, ext):
    extend(j, feat, halo, cs, ext)
    acc = taps[j, 0:1, cs] * ext[j, PAD : PAD + L, :]
    for k in range(1, TAPS):
        acc = acc + taps[j, k : k + 1, cs] * ext[j, pl.ds(PAD - k, L), :]
    return acc


def two_parts(table):
    high = table.astype(BF16).astype(F32)
    both = jnp.concatenate([high, table - high], axis=0)
    return jnp.concatenate([both, both], axis=1).astype(BF16)


def weighted_rows(table, x):
    both = jnp.dot(two_parts(table), split(x), preferred_element_type=F32)
    return both[0:POLES, :] + both[POLES : 2 * POLES, :]


def lane_place():
    return iota((POLES, L), 1).astype(F32)


def spread_poles(lane_rate, sign, rows):
    lane = iota((L, 4 * POLES), 1)
    place = iota((L, 4 * POLES), 0).astype(F32)
    steps = place + 1.0 if sign > 0 else L - 1.0 - place
    table = jnp.exp(-steps * lane_rate[:, 0 : 4 * POLES])
    high = table.astype(BF16).astype(F32)
    left = jnp.where((lane // POLES) % 2 == 0, high, table - high).astype(BF16)
    top = rows.astype(BF16).astype(F32)
    low = rows - top
    right = jnp.concatenate([top, top, low, low], axis=0).astype(BF16)
    return jnp.dot(left, right, preferred_element_type=F32)


def ends_kernel(by_pole, feat, halo, taps, k_o, v_o, e_o, ext):
    def body(gi, cs):
        key = filtered(1, taps, feat, halo, cs, ext)
        value = filtered(2, taps, feat, halo, cs, ext)
        k_o[:, cs] = key
        v_o[:, cs] = value
        e_o[gi] = weighted_rows(jnp.exp(-by_pole[gi] * (L - 1.0 - lane_place())), key * value)

    return body, None


def query_kernel(by_pole, k, v, feat, halo, taps, q_o, deep_o, ext):
    def body(gi, cs):
        q_o[:, cs] = filtered(0, taps, feat, halo, cs, ext)
        lane = lane_place()
        table = (L - 1.0 - lane) * jnp.exp(-by_pole[gi] * (L - 2.0 - lane))
        deep_o[gi] = weighted_rows(table, k[:, cs] * v[:, cs])

    return body, None


def states_kernel(by_pole, k, v, weight, skip, bl_o):
    tri = ones_tri()

    def body(gi, cs):
        prod = k[:, cs] * v[:, cs]
        modal = skip[0:1, cs] * prod
        grow, decay = powers(by_pole[gi], 1.0), powers(by_pole[gi], -1.0)
        for p in range(0, POLES, 2):
            both = tri_dot(tri, [grow[p] * prod, grow[p + 1] * prod])
            for i in range(2):
                state = decay[p + i] * both[:, i * GS : (i + 1) * GS]
                modal = modal + weight[p + i : p + i + 1, cs] * state
        bl_o[:, cs] = modal

    return body, None


def scan_kernel(back, rate, where, rows, *refs):
    me = where[0]
    group = me // 4
    pole = 2 * (me % 4)
    low, high = rate[pole, group], rate[pole + 1, group]
    row, col = iota((L, L), 0), iota((L, L), 1)
    lag = col // 2 - row // 2 - 1 if back else row // 2 - col // 2 - 1
    keep = (lag >= 0) & (row % 2 == col % 2)
    own = jnp.where(row % 2 == 0, low, high)
    decay = jnp.where(keep, jnp.exp(-(own * L) * jnp.maximum(lag, 0).astype(F32)), 0.0)
    refs[-1][...] = jnp.dot(decay, rows[...], precision=HIGHEST, preferred_element_type=F32)


def branch_kernel(q, bl, cot, gain, state_in, by_lane, weight, br_o, stats_o, acc):
    acc[...] = jnp.zeros_like(acc)

    def body(gi, cs):
        branch = bl[:, cs] + spread_poles(by_lane[gi], 1, weight[:, cs] * state_in[gi])
        br_o[:, cs] = branch
        gated = q[:, cs] * branch
        acc[0] += gated * gated
        acc[1] += (gain[0:1, cs] * cot[:, cs].astype(F32)) * gated

    def last():
        row = iota((8, L), 0)
        squares = rowsum(acc[0].T)
        slopes = rowsum(acc[1].T)
        stats_o[...] = jnp.where(row == 0, squares, jnp.where(row == 1, slopes, 0.0))

    return body, last


def down(row):
    return jnp.broadcast_to(row, (L, L)).T


def gate_kernel(stats, q, br, cot, gain, by_pole, g_o, back_o, edge_o):
    inv, pull = row_scales(stats)
    def body(gi, cs):
        query, branch = q[:, cs], br[:, cs]
        dgated = (gain[0:1, cs] * cot[:, cs].astype(F32)) * inv - (query * branch) * pull
        dbranch = dgated * query
        g_o[:, cs] = dbranch
        back = weighted_rows(jnp.exp(-by_pole[gi] * (lane_place() + 1.0)), dbranch)
        back_o[gi] = back
        edge_o[0, :, cs] = dgated[0:PAD, :] * branch[0:PAD, :]
        edge_o[1, :, cs] = back

    return body, None


def adjoint_kernel(
    by_pole, g, k, v, weight, skip, state_in, back, deep, edge,
    dpl_o, res_o, loc_o, mix_o, skip_o, edge_o,
):
    tri = ones_and_lags()
    lane = lane_place()

    def body(gi, cs):
        dbranch = g[:, cs]
        key, value = k[:, cs], v[:, cs]
        prod = key * value
        total = skip[0:1, cs] * dbranch
        skip_o[0:1, cs] = rowsum(dbranch * prod)
        own_in = state_in[gi]
        own_rate = by_pole[gi]
        once = jnp.exp(-own_rate)
        residue = own_in * back[gi]
        heavy = weighted_rows((lane + 1.0) * jnp.exp(-own_rate * lane), dbranch)
        mix_o[gi] = once * (deep[gi] + L * jnp.exp(-(L - 1) * own_rate) * own_in)
        loc = once * own_in * heavy
        grow, decay = powers(own_rate, 1.0), powers(own_rate, -1.0)
        for p in range(0, POLES, 2):
            both = tri_dot(tri, [decay[p] * dbranch, decay[p + 1] * dbranch])
            for i in range(2):
                at = slice(p + i, p + i + 1)
                lanes = slice(i * GS, (i + 1) * GS)
                adjoint = grow[p + i] * both[0:L, lanes]
                total = total + weight[at, cs] * adjoint
                res_o[gi, at, :] = residue[at, :] + rowsum(prod * adjoint)
                loc_o[gi, at, :] = loc[at, :] + rowsum((prod * grow[p + i]) * both[L : 2 * L, lanes])
        dpl_o[:, cs] = total
        edge_o[0, :, cs] = edge[0, :, cs]
        edge_o[1, :, cs] = total[0:PAD, :]
        edge_o[2, :, cs] = edge[1, :, cs]
        edge_o[3, :, cs] = key[0:PAD, :]
        edge_o[4, :, cs] = value[0:PAD, :]

    return body, None


def tap_sums(pack_o, gi, j, own, ext):
    for t in range(TAPS):
        at = TAPS * j + t
        pack_o[gi, at : at + 1, :] = rowsum(own * ext[j, pl.ds(PAD - t, L), :])


def row_scales(stats):
    inv_row = lax.rsqrt(stats[0:1, :] / D + EPSILON)
    return down(inv_row), down(stats[1:2, :] * inv_row * inv_row * inv_row / D)


def outs_kernel(stats, br, cot, gain, res, skips, feat, halo, taps, pack_o, ext):
    inv, pull = row_scales(stats)

    def body(gi, cs):
        branch = br[:, cs]
        grad = cot[:, cs].astype(F32)
        gated = filtered(0, taps, feat, halo, cs, ext) * branch
        dquery = ((gain[0:1, cs] * grad) * inv - gated * pull) * branch
        tap_sums(pack_o, gi, 0, dquery, ext)
        pack_o[gi, 7:21, :] = jnp.zeros((2 * TAPS, GS), F32)
        pack_o[gi, 21:29, :] = res[gi]
        pack_o[gi, 29:30, :] = skips[0:1, cs]
        pack_o[gi, 30:31, :] = rowsum(grad * (gated * inv))
        pack_o[gi, 31:32, :] = jnp.zeros((1, GS), F32)

    return body, None


def sums_kernel(later, by_pole, by_lane, weight, loc, mix, dpl, k, v, feat, halo, pack, pack_o, ext):
    lane, sub = iota((POLES, GS), 1), iota((POLES, GS), 0)

    def body(gi, cs):
        coming = later[gi]
        scaled = weight[:, cs] * coming
        dprod = dpl[:, cs] + spread_poles(by_lane[gi], -1, scaled)
        pack_o[gi] = pack[gi]
        for j, other in ((1, v), (2, k)):
            extend(j, feat, halo, cs, ext)
            tap_sums(pack_o, gi, j, dprod * other[:, cs], ext)
        inner = jnp.sum(weight[:, cs] * loc[gi] + scaled * mix[gi], axis=1, keepdims=True)
        pack_o[gi, 31:32, :] = rowsum(jnp.where(lane == sub, -by_pole[gi] * inner, 0.0))

    return body, None


def finish_kernel(
    rate, later, by_lane, dpl, q, k, v, br, cot, weight, rim, taps, stats, gain, grad_o, out_o, dext
):
    ahead = (iota((PAD, GS), 0) + 1).astype(F32)
    inv, pull = row_scales(stats)

    def body(gi, cs):
        coming = later[gi]
        branch = br[:, cs]
        gated = q[:, cs] * branch
        out_o[:, cs] = (gain[0:1, cs] * (gated * inv)).astype(BF16)
        dprod = dpl[:, cs] + spread_poles(by_lane[gi], -1, weight[:, cs] * coming)
        dext[0, 0:L, :] = ((gain[0:1, cs] * cot[:, cs].astype(F32)) * inv - gated * pull) * branch
        dext[1, 0:L, :] = dprod * v[:, cs]
        dext[2, 0:L, :] = dprod * k[:, cs]
        beyond = weight[:, cs] * (coming - rim[2, :, cs])
        next_prod = rim[1, :, cs]
        for p in range(POLES):
            next_prod = next_prod + jnp.exp(ahead * rate[p, gi]) * beyond[p : p + 1, :]
        dext[0, L : L + PAD, :] = rim[0, :, cs]
        dext[1, L : L + PAD, :] = next_prod * rim[4, :, cs]
        dext[2, L : L + PAD, :] = next_prod * rim[3, :, cs]
        for j in range(3):
            acc = taps[j, 0:1, cs] * dext[j, 0:L, :]
            for t in range(1, TAPS):
                acc = acc + taps[j, t : t + 1, cs] * dext[j, pl.ds(t, L), :]
            grad_o[j, :, cs] = acc.astype(BF16)

    return body, None


def relay_kernel(parts, *refs):
    out = refs[-1]
    out[...] = jnp.broadcast_to(jnp.sum(parts[...], axis=0, keepdims=True), out.shape)


def unpack_kernel(pack, conv_o, rate_o, res_o, skip_o, gain_o):
    groups = pack.shape[0]
    for gi in range(groups):
        cs = slice(gi * GS, (gi + 1) * GS)
        for j in range(3):
            conv_o[j, :, cs] = pack[gi, TAPS * j : TAPS * j + TAPS, :]
        res_o[:, cs] = pack[gi, 21:29, :]
        skip_o[0:1, cs] = pack[gi, 29:30, :]
        gain_o[0:1, cs] = pack[gi, 30:31, :]
    rates = jnp.concatenate([pack[gi, 31:32, :] for gi in range(groups)], axis=0)
    rate_o[...] = rates.T[0:POLES, :]


def smem():
    return pl.BlockSpec(memory_space=pltpu.SMEM)


def vmem():
    return pl.BlockSpec(memory_space=pltpu.VMEM)


def shape(*dims, dtype=F32):
    return jax.ShapeDtypeStruct(dims, dtype)


ends_kernel.kinds = ((W, F12, V, C,), (C, C, G,))
query_kernel.kinds = ((W, C, C, F0, V, C,), (C, G,))
states_kernel.kinds = ((W, C, C, C, C,), (C,))
branch_kernel.kinds = ((C, C, C, C, G, W, C,), (C, W,))
gate_kernel.kinds = ((W, C, C, C, C, W,), (C, G, C,))
adjoint_kernel.kinds = ((W, C, C, C, C, C, G, G, G, C,), (C, G, G, G, C, C,))
outs_kernel.kinds = ((W, C, C, C, G, C, F0, V, C,), (G,))
sums_kernel.kinds = ((G, W, W, C, G, G, C, C, C, F12, V, G,), (G,))
finish_kernel.kinds = ((S, G, W, C, C, C, C, C, C, C, C, C, W, C,), (C, C,))


def shifted(value, step):
    pairs = [(i, i + step) for i in range(64) if 0 <= i + step < 64]
    return lax.ppermute(value, CTX, pairs)


def local(features, conv_weight, log_rate, residues, skip_weight, norm_gain, cotangent):
    feat = features[0].transpose(1, 0, 2)
    taps = conv_weight.transpose(1, 0, 2)
    cot = cotangent[0]
    channels = feat.shape[2]
    groups = log_rate.shape[1]
    count = lax.axis_size(CTX)
    skip = skip_weight[None]
    gain = norm_gain[None]
    where = lax.axis_index(CTX).astype(jnp.int32)[None]

    def call(setup, outs, args, extra=(), flops=0, moved=0, special=0):
        kinds_in, kinds_out = setup.kinds
        fetched = [a for a, k in zip(args, kinds_in) if k not in HELD]
        space = {"smem": pltpu.SMEM, "vmem": pltpu.VMEM}
        return pl.pallas_call(
            functools.partial(streamed, setup, kinds_in, kinds_out),
            in_specs=[pl.BlockSpec(memory_space=space.get(k, pl.ANY)) for k in kinds_in],
            out_specs=[pl.BlockSpec(memory_space=pl.ANY) for _ in outs],
            out_shape=outs,
            scratch_shapes=[pltpu.SemaphoreType.DMA((len(fetched) + len(outs), PARTS))]
            + [pltpu.VMEM(a.shape, a.dtype) for a in [*fetched, *outs]]
            + [pltpu.VMEM(d, F32) for d in extra],
            compiler_params=params({ends_kernel: ENDS_MIB, outs_kernel: OUTS_MIB}.get(setup, VMEM_MIB)),
            cost_estimate=pl.CostEstimate(flops=flops, bytes_accessed=moved, transcendentals=special),
            name=setup.__name__,
        )(*args)

    wide = shape(L, channels)
    per_pole = shape(groups, POLES, GS)
    edges = shape(2, PAD, channels)
    ext3 = (3, PAD + L, GS)

    halo = shifted(feat[:, L - PAD :], 1)
    rate = jnp.exp(log_rate)
    by_pole = jnp.broadcast_to(rate.T[:, :, None], (groups, POLES, GS))
    by_lane = jnp.tile(rate.T, (1, GS // POLES))[:, None, :]

    key, value, ends = call(
        ends_kernel, [wide, wide, per_pole], (by_pole, feat, halo, taps), [ext3]
    )

    def owned(rows):
        return lax.all_to_all(rows.reshape(count, 2, GS), CTX, 0, 0).reshape(L, GS)

    def carried(rows, after, back):
        summed = pl.pallas_call(
            functools.partial(scan_kernel, back),
            in_specs=[smem(), smem(), vmem()] + [pl.BlockSpec(memory_space=pl.ANY)] * len(after),
            out_specs=vmem(),
            out_shape=shape(L, GS),
            compiler_params=params(VMEM_MIB),
            name="carry_back" if back else "carry_on",
        )(rate, where, rows, *after)
        given = lax.all_to_all(summed.reshape(count, 2, GS), CTX, 0, 0)
        return given.reshape(groups, POLES, GS)

    rows_in = owned(ends)
    query, deep = call(
        query_kernel,
        [wide, per_pole],
        (by_pole, key, value, feat, halo, taps),
        [ext3],
        flops=1_000_000_000,
        moved=6_000_000,
    )
    state_in = carried(rows_in, (deep,), False)

    base = call(
        states_kernel,
        [wide],
        (by_pole, key, value, residues, skip),
        flops=4_000_000_000,
        moved=4_000_000,
        special=4_000_000,
    )[0]
    branch, stats = call(
        branch_kernel,
        [wide, shape(8, L)],
        (query, base, cot, gain, state_in, by_lane, residues),
        [(2, L, GS)],
    )
    stats = lax.psum(stats, "c")

    dbranch, back_in, edge = call(
        gate_kernel, [wide, per_pole, edges], (stats, query, branch, cot, gain, by_pole)
    )
    rows_back = owned(back_in)
    dlocal, res_part, loc_part, mix_part, skip_part, edge = call(
        adjoint_kernel,
        [wide, per_pole, per_pole, per_pole, shape(1, channels), shape(5, PAD, channels)],
        (by_pole, dbranch, key, value, residues, skip, state_in, back_in, deep, edge),
        flops=6_000_000_000,
        moved=16_000_000,
        special=4_000_000,
    )
    later = carried(rows_back, (loc_part,), True)
    rim = shifted(edge, -1)

    pack = call(
        outs_kernel,
        [shape(groups, ROWS, GS)],
        (stats, branch, cot, gain, res_part, skip_part, feat, halo, taps),
        [ext3],
        flops=1_000_000_000,
        moved=4_000_000,
    )[0]
    pack = call(
        sums_kernel,
        [shape(groups, ROWS, GS)],
        (later, by_pole, by_lane, residues, loc_part, mix_part, dlocal, key, value, feat, halo, pack),
        [ext3],
    )[0]
    feature_grad, block_out = call(
        finish_kernel,
        [shape(3, L, channels, dtype=BF16), shape(L, channels, dtype=BF16)],
        (rate, later, by_lane, dlocal, query, key, value, branch, cot, residues, rim, taps, stats, gain),
        [ext3],
        flops=1_000_000_000,
        moved=12_000_000,
    )

    def summed_copies(parts, after, name):
        return pl.pallas_call(
            relay_kernel,
            in_specs=[vmem()] + [pl.BlockSpec(memory_space=pl.ANY)] * len(after),
            out_specs=vmem(),
            out_shape=shape(*parts.shape),
            compiler_params=params(VMEM_MIB),
            name=name,
        )(parts, *after)

    owned_rows = summed_copies(lax.all_to_all(pack, YX, 0, 0), (rim,), "add_over_yx")
    everyone = lax.all_to_all(owned_rows, "z", 0, 0)
    totals = lax.all_to_all(summed_copies(everyone, (feature_grad,), "add_over_z"), YX, 0, 0)
    conv, rate_grad, res, skip_grad, gain_grad = pl.pallas_call(
        unpack_kernel,
        out_shape=[shape(3, TAPS, channels), shape(POLES, groups), shape(POLES, channels)] + [shape(1, channels)] * 2,
        compiler_params=params(16),
        name="unpack",
    )(totals)
    return (
        block_out[None],
        feature_grad.transpose(1, 0, 2)[None],
        conv.transpose(1, 0, 2),
        rate_grad,
        res,
        skip_grad[0],
        gain_grad[0],
    )


def solution(mesh):
    split_mesh = Mesh(mesh.devices.reshape(4, 4, 16, 2), ("y", "x", "z", "c"))
    in_specs = (
        P("y", CTX, None, "c"),
        P(None, None, "c"),
        P(None, "c"),
        P(None, "c"),
        P("c"),
        P("c"),
        P("y", CTX, "c"),
    )
    out_specs = (
        P("y", CTX, "c"),
        P("y", CTX, None, "c"),
        P(None, None, "c"),
        P(None, "c"),
        P(None, "c"),
        P("c"),
        P("c"),
    )
    return jax.shard_map(local, mesh=split_mesh, in_specs=in_specs, out_specs=out_specs, check_vma=False)
```

```python
import functools
import jax
import jax.numpy as jnp
from jax import lax
from jax.experimental import pallas as pl
from jax.experimental.pallas import tpu as pltpu
from jax.sharding import Mesh
from jax.sharding import PartitionSpec as P

D = 4096
EPSILON = 1e-06
HIGHEST = lax.Precision.HIGHEST
F32 = jnp.float32
BF16 = jnp.bfloat16
L = 128
GS = 128
POLES = 8
TAPS = 7
PAD = 8
GROUPS_HERE = 16
PARTS = 4
HELD = ("smem", "vmem", "order")
STREAMS = {"first": slice(0, 1), "last": slice(1, 3)}
F0, F12 = "first", "last"
C, G, W, S, V, O = "cols", "groups", "whole", "smem", "vmem", "order"
ROWS = 32
VMEM_MIB = 53
ENDS_MIB = 53.6
OUTS_MIB = 53
CTX = ("x", "z")
YX = ("y", "x")


def window(ref, kind, part):
    if kind == "cols":
        span = ref.shape[-1] // PARTS
        at = pl.ds(pl.multiple_of(part * span, span), span)
        return ref.at[(slice(None),) * (len(ref.shape) - 1) + (at,)]
    if kind in STREAMS:
        span = ref.shape[-1] // PARTS
        return ref.at[STREAMS[kind], :, pl.ds(pl.multiple_of(part * span, span), span)]
    if kind == "groups":
        span = ref.shape[0] // PARTS
        return ref.at[pl.ds(part * span, span)]
    return ref


def streamed(setup, kinds_in, kinds_out, *refs):
    ins, outs = refs[: len(kinds_in)], refs[len(kinds_in) : len(kinds_in) + len(kinds_out)]
    rest = list(refs[len(kinds_in) + len(kinds_out) :])
    sems, scratch = rest[0], rest[1:]
    moved = [k for k in kinds_in if k not in HELD]
    in_bufs = scratch[: len(moved)]
    out_bufs = scratch[len(moved) : len(moved) + len(kinds_out)]
    extra = scratch[len(moved) + len(kinds_out) :]
    sources = [r for r, k in zip(ins, kinds_in) if k not in HELD]

    def fetch(n, part):
        src, dst = window(sources[n], moved[n], part), window(in_bufs[n], moved[n], part)
        return pltpu.make_async_copy(src, dst, sems.at[n, part])

    def store(n, part):
        src, dst = window(out_bufs[n], kinds_out[n], part), window(outs[n], kinds_out[n], part)
        return pltpu.make_async_copy(src, dst, sems.at[len(moved) + n, part])

    for n, kind in enumerate(moved):
        if kind == "whole":
            fetch(n, 0).start()

    def begin(part, carry):
        for n, kind in enumerate(moved):
            if kind != "whole":
                fetch(n, part).start()
        return carry

    lax.fori_loop(0, PARTS, begin, 0)
    for n, kind in enumerate(moved):
        if kind == "whole":
            fetch(n, 0).wait()
    buffers = iter(in_bufs)
    views = [r if k in HELD else next(buffers) for r, k in zip(ins, kinds_in)]
    body, last = setup(*[v for v, k in zip(views, kinds_in) if k != "order"], *out_bufs, *extra)
    per_part = GROUPS_HERE // PARTS

    def step(part, carry):
        for n, kind in enumerate(moved):
            if kind != "whole":
                fetch(n, part).wait()
        for i in range(per_part):
            gi = part * per_part + i
            body(gi, pl.ds(pl.multiple_of(gi * GS, GS), GS))
        for n, kind in enumerate(kinds_out):
            if kind != "whole":
                store(n, part).start()
        return carry

    lax.fori_loop(0, PARTS, step, 0)
    if last is not None:
        last()
    for n, kind in enumerate(kinds_out):
        if kind == "whole":
            store(n, 0).start()

    def end(part, carry):
        for n, kind in enumerate(kinds_out):
            if kind != "whole":
                store(n, part).wait()
        return carry

    lax.fori_loop(0, PARTS, end, 0)
    for n, kind in enumerate(kinds_out):
        if kind == "whole":
            store(n, 0).wait()


def params(mib):
    return pltpu.CompilerParams(vmem_limit_bytes=int(mib * 1024 * 1024))


def iota(shape, dim):
    return lax.broadcasted_iota(jnp.int32, shape, dim)


def ones_tri():
    row = iota((L, 2 * L), 0)
    col = iota((L, 2 * L), 1) % L
    return jnp.where(col <= row, 1.0, 0.0).astype(BF16)


def ones_and_lags():
    row = iota((L, 2 * L), 0)
    col = iota((L, 2 * L), 1) % L
    ones = jnp.where(col >= row, 1.0, 0.0)
    return jnp.concatenate([ones, jnp.maximum(col - row, 0).astype(F32)], axis=0).astype(BF16)


def powers(rates, sign):
    column = iota((PAD, GS), 0).astype(F32)
    spans = [PAD * 2**n for n in range(4)]
    factors = [jnp.exp((sign * span) * rates) for span in spans]
    tables = []
    for p in range(POLES):
        table = jnp.exp((sign * column) * rates[p : p + 1, :])
        for factor in factors:
            table = jnp.concatenate([table, table * factor[p : p + 1, :]], axis=0)
        tables.append(table)
    return tables


def split(x):
    high = x.astype(BF16)
    low = (x - high.astype(F32)).astype(BF16)
    return jnp.concatenate([high, low], axis=0)


def tri_dot(tri, xs):
    return jnp.dot(tri, jnp.concatenate([split(x) for x in xs], axis=1), preferred_element_type=F32)


def rowsum(x):
    return jnp.sum(x, axis=0, keepdims=True)


def extend(j, feat, halo, cs, ext):
    ext[j, 0:PAD, :] = halo[j, :, cs].astype(F32)
    ext[j, PAD : PAD + L, :] = feat[j, :, cs].astype(F32)


def filtered(j, taps, feat, halo, cs, ext):
    extend(j, feat, halo, cs, ext)
    acc = taps[j, 0:1, cs] * ext[j, PAD : PAD + L, :]
    for k in range(1, TAPS):
        acc = acc + taps[j, k : k + 1, cs] * ext[j, pl.ds(PAD - k, L), :]
    return acc


def two_parts(table):
    high = table.astype(BF16).astype(F32)
    both = jnp.concatenate([high, table - high], axis=0)
    return jnp.concatenate([both, both], axis=1).astype(BF16)


def weighted_rows(table, x):
    both = jnp.dot(two_parts(table), split(x), preferred_element_type=F32)
    return both[0:POLES, :] + both[POLES : 2 * POLES, :]


def lane_place():
    return iota((POLES, L), 1).astype(F32)


def spread_poles(lane_rate, sign, rows):
    lane = iota((L, 4 * POLES), 1)
    place = iota((L, 4 * POLES), 0).astype(F32)
    steps = place + 1.0 if sign > 0 else L - 1.0 - place
    table = jnp.exp(-steps * lane_rate[:, 0 : 4 * POLES])
    high = table.astype(BF16).astype(F32)
    left = jnp.where((lane // POLES) % 2 == 0, high, table - high).astype(BF16)
    top = rows.astype(BF16).astype(F32)
    low = rows - top
    right = jnp.concatenate([top, top, low, low], axis=0).astype(BF16)
    return jnp.dot(left, right, preferred_element_type=F32)


def ends_kernel(by_pole, feat, halo, taps, k_o, v_o, e_o, ext):
    def body(gi, cs):
        key = filtered(1, taps, feat, halo, cs, ext)
        value = filtered(2, taps, feat, halo, cs, ext)
        k_o[:, cs] = key
        v_o[:, cs] = value
        e_o[gi] = weighted_rows(jnp.exp(-by_pole[gi] * (L - 1.0 - lane_place())), key * value)

    return body, None


def query_kernel(by_pole, k, v, feat, halo, taps, q_o, deep_o, ext):
    def body(gi, cs):
        q_o[:, cs] = filtered(0, taps, feat, halo, cs, ext)
        lane = lane_place()
        table = (L - 1.0 - lane) * jnp.exp(-by_pole[gi] * (L - 2.0 - lane))
        deep_o[gi] = weighted_rows(table, k[:, cs] * v[:, cs])

    return body, None


def states_kernel(by_pole, k, v, weight, skip, bl_o):
    tri = ones_tri()

    def body(gi, cs):
        prod = k[:, cs] * v[:, cs]
        modal = skip[0:1, cs] * prod
        grow, decay = powers(by_pole[gi], 1.0), powers(by_pole[gi], -1.0)
        for p in range(0, POLES, 2):
            both = tri_dot(tri, [grow[p] * prod, grow[p + 1] * prod])
            for i in range(2):
                state = decay[p + i] * both[:, i * GS : (i + 1) * GS]
                modal = modal + weight[p + i : p + i + 1, cs] * state
        bl_o[:, cs] = modal

    return body, None


def scan_kernel(back, rate, where, rows, *refs):
    me = where[0]
    group = me // 4
    pole = 2 * (me % 4)
    low, high = rate[pole, group], rate[pole + 1, group]
    row, col = iota((L, L), 0), iota((L, L), 1)
    lag = col // 2 - row // 2 - 1 if back else row // 2 - col // 2 - 1
    keep = (lag >= 0) & (row % 2 == col % 2)
    own = jnp.where(row % 2 == 0, low, high)
    decay = jnp.where(keep, jnp.exp(-(own * L) * jnp.maximum(lag, 0).astype(F32)), 0.0)
    high = decay.astype(BF16)
    low = (decay - high.astype(F32)).astype(BF16)
    both = split(rows[...])
    left = jnp.concatenate([high, high, low], axis=1)
    right = jnp.concatenate([both, both[0:L, :]], axis=0)
    refs[-1][...] = jnp.dot(left, right, preferred_element_type=F32)


def branch_kernel(q, bl, cot, gain, state_in, by_lane, weight, br_o, stats_o, acc):
    acc[...] = jnp.zeros_like(acc)

    def body(gi, cs):
        branch = bl[:, cs] + spread_poles(by_lane[gi], 1, weight[:, cs] * state_in[gi])
        br_o[:, cs] = branch
        gated = q[:, cs] * branch
        acc[0] += gated * gated
        acc[1] += (gain[0:1, cs] * cot[:, cs].astype(F32)) * gated

    def last():
        row = iota((8, L), 0)
        squares = rowsum(acc[0].T)
        slopes = rowsum(acc[1].T)
        stats_o[...] = jnp.where(row == 0, squares, jnp.where(row == 1, slopes, 0.0))

    return body, last


def down(row):
    return jnp.broadcast_to(row, (L, L)).T


def gate_kernel(stats, q, br, cot, gain, by_pole, g_o, back_o, edge_o):
    inv, pull = row_scales(stats)
    def body(gi, cs):
        query, branch = q[:, cs], br[:, cs]
        dgated = (gain[0:1, cs] * cot[:, cs].astype(F32)) * inv - (query * branch) * pull
        dbranch = dgated * query
        g_o[:, cs] = dbranch
        back = weighted_rows(jnp.exp(-by_pole[gi] * (lane_place() + 1.0)), dbranch)
        back_o[gi] = back
        edge_o[0, :, cs] = dgated[0:PAD, :] * branch[0:PAD, :]
        edge_o[1, :, cs] = back

    return body, None


def adjoint_kernel(
    by_pole, g, k, v, weight, skip, state_in, back, deep, edge,
    dpl_o, res_o, loc_o, mix_o, skip_o, edge_o,
):
    tri = ones_and_lags()
    lane = lane_place()

    def body(gi, cs):
        dbranch = g[:, cs]
        key, value = k[:, cs], v[:, cs]
        prod = key * value
        total = skip[0:1, cs] * dbranch
        skip_o[0:1, cs] = rowsum(dbranch * prod)
        own_in = state_in[gi]
        own_rate = by_pole[gi]
        once = jnp.exp(-own_rate)
        residue = own_in * back[gi]
        heavy = weighted_rows((lane + 1.0) * jnp.exp(-own_rate * lane), dbranch)
        mix_o[gi] = once * (deep[gi] + L * jnp.exp(-(L - 1) * own_rate) * own_in)
        loc = once * own_in * heavy
        grow, decay = powers(own_rate, 1.0), powers(own_rate, -1.0)
        for p in range(0, POLES, 2):
            both = tri_dot(tri, [decay[p] * dbranch, decay[p + 1] * dbranch])
            for i in range(2):
                at = slice(p + i, p + i + 1)
                lanes = slice(i * GS, (i + 1) * GS)
                adjoint = grow[p + i] * both[0:L, lanes]
                total = total + weight[at, cs] * adjoint
                res_o[gi, at, :] = residue[at, :] + rowsum(prod * adjoint)
                loc_o[gi, at, :] = loc[at, :] + rowsum((prod * grow[p + i]) * both[L : 2 * L, lanes])
        dpl_o[:, cs] = total
        edge_o[0, :, cs] = edge[0, :, cs]
        edge_o[1, :, cs] = total[0:PAD, :]
        edge_o[2, :, cs] = edge[1, :, cs]
        edge_o[3, :, cs] = key[0:PAD, :]
        edge_o[4, :, cs] = value[0:PAD, :]

    return body, None


def tap_sums(pack_o, gi, j, own, ext):
    for t in range(TAPS):
        at = TAPS * j + t
        pack_o[gi, at : at + 1, :] = rowsum(own * ext[j, pl.ds(PAD - t, L), :])


def row_scales(stats):
    inv_row = lax.rsqrt(stats[0:1, :] / D + EPSILON)
    return down(inv_row), down(stats[1:2, :] * inv_row * inv_row * inv_row / D)


def outs_kernel(stats, br, cot, gain, res, skips, feat, halo, taps, pack_o, ext):
    inv, pull = row_scales(stats)

    def body(gi, cs):
        branch = br[:, cs]
        grad = cot[:, cs].astype(F32)
        gated = filtered(0, taps, feat, halo, cs, ext) * branch
        dquery = ((gain[0:1, cs] * grad) * inv - gated * pull) * branch
        tap_sums(pack_o, gi, 0, dquery, ext)
        pack_o[gi, 7:21, :] = jnp.zeros((2 * TAPS, GS), F32)
        pack_o[gi, 21:29, :] = res[gi]
        pack_o[gi, 29:30, :] = skips[0:1, cs]
        pack_o[gi, 30:31, :] = rowsum(grad * (gated * inv))
        pack_o[gi, 31:32, :] = jnp.zeros((1, GS), F32)

    return body, None


def sums_kernel(later, by_pole, by_lane, weight, loc, mix, dpl, k, v, feat, halo, pack, pack_o, ext):
    lane, sub = iota((POLES, GS), 1), iota((POLES, GS), 0)

    def body(gi, cs):
        coming = later[gi]
        scaled = weight[:, cs] * coming
        dprod = dpl[:, cs] + spread_poles(by_lane[gi], -1, scaled)
        pack_o[gi] = pack[gi]
        for j, other in ((1, v), (2, k)):
            extend(j, feat, halo, cs, ext)
            tap_sums(pack_o, gi, j, dprod * other[:, cs], ext)
        inner = jnp.sum(weight[:, cs] * loc[gi] + scaled * mix[gi], axis=1, keepdims=True)
        pack_o[gi, 31:32, :] = rowsum(jnp.where(lane == sub, -by_pole[gi] * inner, 0.0))

    return body, None


def finish_kernel(
    rate, later, by_lane, dpl, q, k, v, br, cot, weight, rim, taps, stats, gain, grad_o, out_o, dext
):
    ahead = (iota((PAD, GS), 0) + 1).astype(F32)
    inv, pull = row_scales(stats)

    def body(gi, cs):
        coming = later[gi]
        branch = br[:, cs]
        gated = q[:, cs] * branch
        out_o[:, cs] = (gain[0:1, cs] * (gated * inv)).astype(BF16)
        dprod = dpl[:, cs] + spread_poles(by_lane[gi], -1, weight[:, cs] * coming)
        dext[0, 0:L, :] = ((gain[0:1, cs] * cot[:, cs].astype(F32)) * inv - gated * pull) * branch
        dext[1, 0:L, :] = dprod * v[:, cs]
        dext[2, 0:L, :] = dprod * k[:, cs]
        beyond = weight[:, cs] * (coming - rim[2, :, cs])
        next_prod = rim[1, :, cs]
        for p in range(POLES):
            next_prod = next_prod + jnp.exp(ahead * rate[p, gi]) * beyond[p : p + 1, :]
        dext[0, L : L + PAD, :] = rim[0, :, cs]
        dext[1, L : L + PAD, :] = next_prod * rim[4, :, cs]
        dext[2, L : L + PAD, :] = next_prod * rim[3, :, cs]
        for j in range(3):
            acc = taps[j, 0:1, cs] * dext[j, 0:L, :]
            for t in range(1, TAPS):
                acc = acc + taps[j, t : t + 1, cs] * dext[j, pl.ds(t, L), :]
            grad_o[j, :, cs] = acc.astype(BF16)

    return body, None


def relay_kernel(parts, *refs):
    out = refs[-1]
    out[...] = jnp.broadcast_to(jnp.sum(parts[...], axis=0, keepdims=True), out.shape)


def unpack_kernel(pack, conv_o, rate_o, res_o, skip_o, gain_o):
    groups = pack.shape[0]
    for gi in range(groups):
        cs = slice(gi * GS, (gi + 1) * GS)
        for j in range(3):
            conv_o[j, :, cs] = pack[gi, TAPS * j : TAPS * j + TAPS, :]
        res_o[:, cs] = pack[gi, 21:29, :]
        skip_o[0:1, cs] = pack[gi, 29:30, :]
        gain_o[0:1, cs] = pack[gi, 30:31, :]
    rates = jnp.concatenate([pack[gi, 31:32, :] for gi in range(groups)], axis=0)
    rate_o[...] = rates.T[0:POLES, :]


def smem():
    return pl.BlockSpec(memory_space=pltpu.SMEM)


def vmem():
    return pl.BlockSpec(memory_space=pltpu.VMEM)


def shape(*dims, dtype=F32):
    return jax.ShapeDtypeStruct(dims, dtype)


ends_kernel.kinds = ((W, F12, V, C,), (C, C, G,))
query_kernel.kinds = ((W, C, C, F0, V, C,), (C, G,))
states_kernel.kinds = ((W, C, C, C, C,), (C,))
branch_kernel.kinds = ((C, C, C, C, G, W, C,), (C, W,))
gate_kernel.kinds = ((W, C, C, C, C, W,), (C, G, C,))
adjoint_kernel.kinds = ((W, C, C, C, C, C, G, G, G, C,), (C, G, G, G, C, C,))
outs_kernel.kinds = ((W, C, C, C, G, C, F0, V, C,), (G,))
sums_kernel.kinds = ((G, W, W, C, G, G, C, C, C, F12, V, G,), (G,))
finish_kernel.kinds = ((S, G, W, C, C, C, C, C, C, C, C, C, W, C,), (C, C,))


def shifted(value, step):
    pairs = [(i, i + step) for i in range(64) if 0 <= i + step < 64]
    return lax.ppermute(value, CTX, pairs)


def local(features, conv_weight, log_rate, residues, skip_weight, norm_gain, cotangent):
    feat = features[0].transpose(1, 0, 2)
    taps = conv_weight.transpose(1, 0, 2)
    cot = cotangent[0]
    channels = feat.shape[2]
    groups = log_rate.shape[1]
    count = lax.axis_size(CTX)
    skip = skip_weight[None]
    gain = norm_gain[None]
    where = lax.axis_index(CTX).astype(jnp.int32)[None]

    def call(setup, outs, args, extra=(), flops=0, moved=0, special=0):
        kinds_in, kinds_out = setup.kinds
        fetched = [a for a, k in zip(args, kinds_in) if k not in HELD]
        space = {"smem": pltpu.SMEM, "vmem": pltpu.VMEM}
        return pl.pallas_call(
            functools.partial(streamed, setup, kinds_in, kinds_out),
            in_specs=[pl.BlockSpec(memory_space=space.get(k, pl.ANY)) for k in kinds_in],
            out_specs=[pl.BlockSpec(memory_space=pl.ANY) for _ in outs],
            out_shape=outs,
            scratch_shapes=[pltpu.SemaphoreType.DMA((len(fetched) + len(outs), PARTS))]
            + [pltpu.VMEM(a.shape, a.dtype) for a in [*fetched, *outs]]
            + [pltpu.VMEM(d, F32) for d in extra],
            compiler_params=params({ends_kernel: ENDS_MIB, outs_kernel: OUTS_MIB}.get(setup, VMEM_MIB)),
            cost_estimate=pl.CostEstimate(flops=flops, bytes_accessed=moved, transcendentals=special),
            name=setup.__name__,
        )(*args)

    wide = shape(L, channels)
    per_pole = shape(groups, POLES, GS)
    edges = shape(2, PAD, channels)
    ext3 = (3, PAD + L, GS)

    halo = shifted(feat[:, L - PAD :], 1)
    rate = jnp.exp(log_rate)
    by_pole = jnp.broadcast_to(rate.T[:, :, None], (groups, POLES, GS))
    by_lane = jnp.tile(rate.T, (1, GS // POLES))[:, None, :]

    key, value, ends = call(
        ends_kernel, [wide, wide, per_pole], (by_pole, feat, halo, taps), [ext3]
    )

    def owned(rows):
        return lax.all_to_all(rows.reshape(count, 2, GS), CTX, 0, 0).reshape(L, GS)

    def carried(rows, after, back):
        summed = pl.pallas_call(
            functools.partial(scan_kernel, back),
            in_specs=[smem(), smem(), vmem()] + [pl.BlockSpec(memory_space=pl.ANY)] * len(after),
            out_specs=vmem(),
            out_shape=shape(L, GS),
            compiler_params=params(VMEM_MIB),
            name="carry_back" if back else "carry_on",
        )(rate, where, rows, *after)
        given = lax.all_to_all(summed.reshape(count, 2, GS), CTX, 0, 0)
        return given.reshape(groups, POLES, GS)

    rows_in = owned(ends)
    query, deep = call(
        query_kernel,
        [wide, per_pole],
        (by_pole, key, value, feat, halo, taps),
        [ext3],
        flops=1_000_000_000,
        moved=6_000_000,
    )
    state_in = carried(rows_in, (deep,), False)

    base = call(
        states_kernel,
        [wide],
        (by_pole, key, value, residues, skip),
        flops=4_000_000_000,
        moved=4_000_000,
        special=4_000_000,
    )[0]
    branch, stats = call(
        branch_kernel,
        [wide, shape(8, L)],
        (query, base, cot, gain, state_in, by_lane, residues),
        [(2, L, GS)],
    )
    stats = lax.psum(stats, "c")

    dbranch, back_in, edge = call(
        gate_kernel, [wide, per_pole, edges], (stats, query, branch, cot, gain, by_pole)
    )
    rows_back = owned(back_in)
    dlocal, res_part, loc_part, mix_part, skip_part, edge = call(
        adjoint_kernel,
        [wide, per_pole, per_pole, per_pole, shape(1, channels), shape(5, PAD, channels)],
        (by_pole, dbranch, key, value, residues, skip, state_in, back_in, deep, edge),
        flops=6_000_000_000,
        moved=16_000_000,
        special=4_000_000,
    )
    later = carried(rows_back, (loc_part,), True)
    rim = shifted(edge, -1)

    pack = call(
        outs_kernel,
        [shape(groups, ROWS, GS)],
        (stats, branch, cot, gain, res_part, skip_part, feat, halo, taps),
        [ext3],
        flops=1_000_000_000,
        moved=4_000_000,
    )[0]
    pack = call(
        sums_kernel,
        [shape(groups, ROWS, GS)],
        (later, by_pole, by_lane, residues, loc_part, mix_part, dlocal, key, value, feat, halo, pack),
        [ext3],
    )[0]
    feature_grad, block_out = call(
        finish_kernel,
        [shape(3, L, channels, dtype=BF16), shape(L, channels, dtype=BF16)],
        (rate, later, by_lane, dlocal, query, key, value, branch, cot, residues, rim, taps, stats, gain),
        [ext3],
        flops=1_000_000_000,
        moved=12_000_000,
    )

    def summed_copies(parts, after, name):
        return pl.pallas_call(
            relay_kernel,
            in_specs=[vmem()] + [pl.BlockSpec(memory_space=pl.ANY)] * len(after),
            out_specs=vmem(),
            out_shape=shape(*parts.shape),
            compiler_params=params(VMEM_MIB),
            name=name,
        )(parts, *after)

    owned_rows = summed_copies(lax.all_to_all(pack, YX, 0, 0), (rim,), "add_over_yx")
    everyone = lax.all_to_all(owned_rows, "z", 0, 0)
    totals = lax.all_to_all(summed_copies(everyone, (feature_grad,), "add_over_z"), YX, 0, 0)
    conv, rate_grad, res, skip_grad, gain_grad = pl.pallas_call(
        unpack_kernel,
        out_shape=[shape(3, TAPS, channels), shape(POLES, groups), shape(POLES, channels)] + [shape(1, channels)] * 2,
        compiler_params=params(16),
        name="unpack",
    )(totals)
    return (
        block_out[None],
        feature_grad.transpose(1, 0, 2)[None],
        conv.transpose(1, 0, 2),
        rate_grad,
        res,
        skip_grad[0],
        gain_grad[0],
    )


def solution(mesh):
    split_mesh = Mesh(mesh.devices.reshape(4, 4, 16, 2), ("y", "x", "z", "c"))
    in_specs = (
        P("y", CTX, None, "c"),
        P(None, None, "c"),
        P(None, "c"),
        P(None, "c"),
        P("c"),
        P("c"),
        P("y", CTX, "c"),
    )
    out_specs = (
        P("y", CTX, "c"),
        P("y", CTX, None, "c"),
        P(None, None, "c"),
        P(None, "c"),
        P(None, "c"),
        P("c"),
        P("c"),
    )
    return jax.shard_map(local, mesh=split_mesh, in_specs=in_specs, out_specs=out_specs, check_vma=False)
```
